512 devices in a mesh: blk: 128 (over y_lo, z, x), rep: 4 (over y_hi, core).
Axes of the slice: x: 4, y: 8 (y_hi: 2, y_lo: 4; y = y_hi * 4 + y_lo), z: 8, core: 2. Of those that a mesh axis runs over, the one named last changes fastest.
Arguments:
- frames: float32 [16384, 3, 1024], P(('blk', 'rep')), may hold values from -25 to 25
Outputs:
- deviation: float32 [16384, 384], P(('blk', 'rep'))
The draws below stay inside these ranges and needn't reach their ends.
All inputs are finite; a program needn't handle non-finite values.
Results may differ from the reference program's by a relative error of at most 0.0003.
Values sent between devices are 32-bit elements; how exact they have to be, the bound alone decides.
No kernel may reach another device: no remote copies, remote signals or barrier semaphores. Data moves between devices by JAX's collectives and lax.ppermute only.
A program may use at most 64 MiB of HBM per device.

```python
import math
import jax
import jax.numpy as jnp
from jax import lax

ATOMS = 1024
REACH = 1
ITERS = 8
BLOCK = 128
BLOCKS = 128
FRAMES = 16384
WINDOW = 384


def draw_frames(key, part):
    key = jax.random.fold_in(key, 11)
    keys = jax.random.split(key, 6)
    axis_scale = jnp.array([1.0, 0.6, 0.3], jnp.float32)
    base = jnp.clip(jax.random.normal(keys[0], (3, ATOMS), jnp.float32), -4.0, 4.0) * axis_scale[:, None]
    flexible = jnp.exp(jax.random.uniform(keys[1], (ATOMS,), jnp.float32, math.log(0.5), 0.0))
    amplitude = jnp.exp(jax.random.uniform(keys[2], (FRAMES, 1, 1), jnp.float32, math.log(0.5), math.log(1.5)))
    noise = jnp.clip(jax.random.normal(keys[3], (FRAMES, 3, ATOMS), jnp.float32), -4.0, 4.0)
    moved = base[None] + amplitude * flexible[None, None, :] * noise
    angles = jax.random.uniform(keys[4], (FRAMES, 3), jnp.float32, -math.pi, math.pi)
    cos_a = jnp.cos(angles[:, 0])
    sin_a = jnp.sin(angles[:, 0])
    cos_b = jnp.cos(angles[:, 1])
    sin_b = jnp.sin(angles[:, 1])
    cos_c = jnp.cos(angles[:, 2])
    sin_c = jnp.sin(angles[:, 2])
    rotation = [[cos_a * cos_b * cos_c - sin_a * sin_c, -cos_a * cos_b * sin_c - sin_a * cos_c, cos_a * sin_b], [sin_a * cos_b * cos_c + cos_a * sin_c, -sin_a * cos_b * sin_c + cos_a * cos_c, sin_a * sin_b], [-sin_b * cos_c, sin_b * sin_c, cos_b]]
    rotated = []
    for row in range(3):
        rotated.append(rotation[row][0][:, None] * moved[:, 0, :] + rotation[row][1][:, None] * moved[:, 1, :] + rotation[row][2][:, None] * moved[:, 2, :])
    placed = jnp.stack(rotated, axis=1)
    offsets = jax.random.uniform(keys[5], (FRAMES, 3, 1), jnp.float32, -3.0, 3.0)
    return (placed + offsets).astype(jnp.float32)


def setup_inputs(seed: int = 0) -> dict:
    seeds = jax.random.split(jax.random.key(seed), 2)
    return {
        "frames": draw_frames(jax.random.fold_in(seeds[1], 71), 0),
    }


def centre(frames):
    return frames - lax.optimization_barrier(jnp.mean(frames, axis=2, keepdims=True))

def square_norms(centred):
    return lax.optimization_barrier(jnp.sum(centred * centred, axis=(1, 2)))

def polar_trace(covariance, scaling):
    iterate = covariance * scaling
    for sweep in range(ITERS):
        gram_matrix = iterate[0][:, None] * iterate[0][None, :] + iterate[1][:, None] * iterate[1][None, :] + iterate[2][:, None] * iterate[2][None, :]
        product = iterate[:, 0][:, None] * gram_matrix[0][None, :] + iterate[:, 1][:, None] * gram_matrix[1][None, :] + iterate[:, 2][:, None] * gram_matrix[2][None, :]
        iterate = 0.5 * (3.0 * iterate - product)
    return lax.optimization_barrier(jnp.sum(iterate * covariance, axis=(0, 1)))

def pair_deviation(resident, resident_norm, visitor):
    atom_count = resident.shape[2]
    row_count = resident.shape[0]
    partner_count = visitor.shape[0]
    visitor_norm = square_norms(visitor)
    products = lax.dot_general(resident.reshape(row_count * 3, atom_count), visitor.reshape(partner_count * 3, atom_count), (((1,), (1,)), ((), ())), precision=lax.Precision.HIGHEST, preferred_element_type=jnp.float32)
    covariance = products.reshape(row_count, 3, partner_count, 3).transpose(1, 3, 0, 2)
    inverse_root = 1.0 / jnp.sqrt(resident_norm + 1e-06)
    partner_root = 1.0 / jnp.sqrt(visitor_norm + 1e-06)
    scaling = inverse_root[:, None] * partner_root[None, :]
    aligned = polar_trace(covariance, scaling)
    return (resident_norm[:, None] + visitor_norm[None, :] - 2.0 * aligned) / atom_count

def reference(frames):
    centred = centre(frames)
    norms_all = square_norms(centred)

    def one_block(block_index):
        first_row = (block_index * BLOCK).astype(jnp.int32)
        resident = lax.dynamic_slice_in_dim(centred, first_row, BLOCK, 0)
        resident_norm = lax.dynamic_slice_in_dim(norms_all, first_row, BLOCK, 0)
        columns = []
        for distance in range(-REACH, REACH + 1):
            partner_first = ((block_index + distance) % BLOCKS * BLOCK).astype(jnp.int32)
            visitor = lax.dynamic_slice_in_dim(centred, partner_first, BLOCK, 0)
            columns.append(pair_deviation(resident, resident_norm, visitor))
        return jnp.concatenate(columns, axis=1)
    tiles = lax.map(one_block, jnp.arange(BLOCKS, dtype=jnp.int32))
    return tiles.reshape(FRAMES, WINDOW)
```

```python
import functools

import jax
import jax.numpy as jnp
from jax import lax
from jax.experimental import pallas as pl
from jax.experimental.pallas import tpu as pltpu
from jax.sharding import PartitionSpec as P

ITERS = 8
ATOMS = 1024
AXES = ("blk", "rep")
CHIPS = 256


def device_of(chip, core):
    half, block = divmod(chip % CHIPS, CHIPS // 2)
    return block * 4 + half * 2 + core


def moved(value, chips, cores):
    pairs = [
        (device_of(chip, core), device_of(chip + chips, (core + cores) % 2))
        for chip in range(CHIPS)
        for core in range(2)
    ]
    return lax.ppermute(value, AXES, pairs)


def centred_of(raw):
    return raw - jnp.sum(raw, axis=1, keepdims=True) * (1.0 / ATOMS)


def split(value):
    high = value.astype(jnp.bfloat16)
    low = (value - high.astype(jnp.float32)).astype(jnp.bfloat16)
    return high, low


def prepare_kernel(core_ref, z0, z1, a0, a1, b0, b1, high_ref, low_ref, norm_ref, column_ref):
    core = core_ref[0]
    column_ref[...] = jnp.zeros_like(column_ref)
    for place, pair in enumerate(((z0, z1), (a0, a1), (b0, b1))):
        for other, ref in enumerate(pair):
            at = core if other == 0 else 1 - core
            start = pl.multiple_of(64 * place + 32 * at, 32)
            norm = jnp.zeros((32, 1), jnp.float32)
            for b in range(3):
                centred = centred_of(ref[32 * b : 32 * b + 32, :])
                norm = norm + jnp.sum(centred * centred, axis=1, keepdims=True)
                high, low = split(centred)
                high_ref[b, pl.ds(start, 32), :] = high
                low_ref[b, pl.ds(start, 32), :] = low
            column_ref[pl.ds(start, 32), :] = jnp.broadcast_to(norm, (32, 128))
    for b in range(3):
        high_ref[b, 192:256, :] = jnp.zeros((64, ATOMS), jnp.bfloat16)
        low_ref[b, 192:256, :] = jnp.zeros((64, ATOMS), jnp.bfloat16)
    norm_ref[...] = jnp.transpose(column_ref[...])[0:8, :]


def polar_trace(cov, scale):
    x = [[cov[a][b] * scale for b in range(3)] for a in range(3)]
    for _ in range(ITERS):
        m = {}
        for p in range(3):
            for q in range(p, 3):
                g = x[0][p] * x[0][q] + x[1][p] * x[1][q] + x[2][p] * x[2][q]
                m[p, q] = m[q, p] = 1.5 - 0.5 * g if p == q else -0.5 * g
        x = [[x[a][0] * m[0, b] + x[a][1] * m[1, b] + x[a][2] * m[2, b] for b in range(3)] for a in range(3)]
    return sum(x[a][b] * cov[a][b] for a in range(3) for b in range(3))


def rows_kernel(rows_ref, high_ref, low_ref, norm_ref, out_ref, left_ref, cov_ref):
    norm = jnp.zeros((32, 1), jnp.float32)
    for a in range(3):
        centred = centred_of(rows_ref[32 * a : 32 * a + 32, :])
        norm = norm + jnp.sum(centred * centred, axis=1, keepdims=True)
        high, low = split(centred)
        left_ref[32 * a : 32 * a + 32, :] = high
        left_ref[96 + 32 * a : 128 + 32 * a, :] = low
    dims = (((1,), (1,)), ((), ()))
    for b in range(3):
        one = lax.dot_general(left_ref[...], high_ref[b], dims, preferred_element_type=jnp.float32)
        two = lax.dot_general(left_ref[...], low_ref[b], dims, preferred_element_type=jnp.float32)
        cov_ref[b] = one[:96] + (one[96:] + two[:96] + two[96:])
    row_root = 1.0 / jnp.sqrt(norm + 1e-6)
    tiles = []
    for t in range(2):
        lanes = slice(128 * t, 128 * t + 128)
        columns = norm_ref[0:1, lanes]
        scale = row_root * (1.0 / jnp.sqrt(columns + 1e-6))
        cov = [[cov_ref[b, 32 * a : 32 * a + 32, lanes] for b in range(3)] for a in range(3)]
        aligned = polar_trace(cov, scale)
        tiles.append((norm + columns - 2.0 * aligned) * (1.0 / ATOMS))
    prev, own, nxt = tiles[0][:, :64], tiles[0][:, 64:], tiles[1][:, :64]
    out_ref[...] = jnp.concatenate([prev, prev, own, own, nxt, nxt], axis=1)


def prepare(core, *frames):
    spec = pl.BlockSpec(memory_space=pltpu.VMEM)
    return pl.pallas_call(
        prepare_kernel,
        out_shape=(
            jax.ShapeDtypeStruct((3, 256, ATOMS), jnp.bfloat16),
            jax.ShapeDtypeStruct((3, 256, ATOMS), jnp.bfloat16),
            jax.ShapeDtypeStruct((8, 256), jnp.float32),
        ),
        in_specs=[pl.BlockSpec(memory_space=pltpu.SMEM)] + [spec] * 6,
        out_specs=(spec, spec, spec),
        scratch_shapes=[pltpu.VMEM((256, 128), jnp.float32)],
        compiler_params=pltpu.CompilerParams(vmem_limit_bytes=32 << 20),
        name="prepare",
    )(core, *frames)


def deviations(rows, high, low, norm, name):
    spec = pl.BlockSpec(memory_space=pltpu.VMEM)
    return pl.pallas_call(
        rows_kernel,
        out_shape=jax.ShapeDtypeStruct((32, 384), jnp.float32),
        in_specs=[spec] * 4,
        out_specs=spec,
        scratch_shapes=[pltpu.VMEM((192, ATOMS), jnp.bfloat16), pltpu.VMEM((3, 96, 256), jnp.float32)],
        compiler_params=pltpu.CompilerParams(vmem_limit_bytes=32 << 20),
        name=name,
    )(rows, high, low, norm)


def on_device(frames):
    rep = lax.axis_index("rep")
    half, core = rep // 2, rep % 2
    chip = half * (CHIPS // 2) + lax.axis_index("blk")
    raw = frames.transpose(1, 0, 2).reshape(96, ATOMS)
    far = moved(raw, CHIPS // 2, 0)
    nxt = moved(raw, -1, 0)
    prv = moved(raw, 1, 0)
    raw_other = moved(raw, 0, 1)
    nxt_other = moved(nxt, 0, 1)
    prv_other = moved(prv, 0, 1)
    high, low, norm = prepare(
        core.reshape(1).astype(jnp.int32), prv, prv_other, raw, raw_other, nxt, nxt_other
    )
    for_partner = deviations(far, high, low, norm, "rows_of_partner")
    returned = moved(for_partner, CHIPS // 2, 0)
    own = deviations(raw, high, low, norm, "rows_of_own")
    lane = lax.broadcasted_iota(jnp.int32, (1, 384), 1)
    column_chip = (chip + CHIPS - 1 + lane // 128) % CHIPS
    here = column_chip // (CHIPS // 2) == lane // 64 % 2
    return jnp.where(here, own, returned)


def solution(mesh):
    return jax.shard_map(
        on_device,
        mesh=mesh,
        in_specs=(P(AXES, None, None),),
        out_specs=P(AXES, None),
        check_vma=False,
    )
```

```python
import functools

import jax
import jax.numpy as jnp
from jax import lax
from jax.experimental import pallas as pl
from jax.experimental.pallas import tpu as pltpu
from jax.sharding import PartitionSpec as P

ITERS = 8
ATOMS = 1024
AXES = ("blk", "rep")
CHIPS = 256
PLANE = 32


def device_of(chip, core):
    half, block = divmod(chip % CHIPS, CHIPS // 2)
    return block * 4 + half * 2 + core


def moved(value, chips, cores, senders=range(CHIPS)):
    pairs = [
        (device_of(chip, core), device_of(chip + chips, (core + cores) % 2))
        for chip in senders
        for core in range(2)
    ]
    return lax.ppermute(value, AXES, pairs)


def centred_of(raw):
    return raw - jnp.sum(raw, axis=1, keepdims=True) * (1.0 / ATOMS)


def split(value):
    high = value.astype(jnp.bfloat16)
    low = (value - high.astype(jnp.float32)).astype(jnp.bfloat16)
    return high, low


def prepare_kernel(core_ref, *refs):
    frames, (high_ref, low_ref, norm_ref, column_ref) = refs[:6], refs[6:]
    core = core_ref[0]
    column_ref[...] = jnp.zeros_like(column_ref)
    for n, ref in enumerate(frames):
        at = core if n % 2 == 0 else 1 - core
        start = pl.multiple_of(64 * (n // 2) + 32 * at, 32)
        norm = jnp.zeros((32, 1), jnp.float32)
        for b in range(3):
            centred = centred_of(ref[32 * b : 32 * b + 32, :])
            norm = norm + jnp.sum(centred * centred, axis=1, keepdims=True)
            high, low = split(centred)
            high_ref[b, pl.ds(start, 32), :] = high
            low_ref[b, pl.ds(start, 32), :] = low
        column_ref[pl.ds(start, 32), :] = jnp.broadcast_to(norm, (32, 128))
    for b in range(3):
        high_ref[b, 192:256, :] = jnp.zeros((64, ATOMS), jnp.bfloat16)
        low_ref[b, 192:256, :] = jnp.zeros((64, ATOMS), jnp.bfloat16)
    norm_ref[...] = jnp.transpose(column_ref[...])[0:8, :]


def polar_trace(cov, scale):
    x = [[cov[a][b] * scale for b in range(3)] for a in range(3)]
    for _ in range(ITERS):
        m = {}
        for p in range(3):
            for q in range(p, 3):
                g = x[0][p] * x[0][q] + x[1][p] * x[1][q] + x[2][p] * x[2][q]
                m[p, q] = m[q, p] = 1.5 - 0.5 * g if p == q else -0.5 * g
        x = [[x[a][0] * m[0, b] + x[a][1] * m[1, b] + x[a][2] * m[2, b] for b in range(3)] for a in range(3)]
    return sum(x[a][b] * cov[a][b] for a in range(3) for b in range(3))


def fill_rows(rows_ref, high_ref, low_ref, norm_ref, out_ref, left_ref, cov_ref):
    norm = jnp.zeros((32, 1), jnp.float32)
    for a in range(3):
        centred = centred_of(rows_ref[32 * a : 32 * a + 32, :])
        norm = norm + jnp.sum(centred * centred, axis=1, keepdims=True)
        high, low = split(centred)
        left_ref[32 * a : 32 * a + 32, :] = high
        left_ref[96 + 32 * a : 128 + 32 * a, :] = low
    dims = (((1,), (1,)), ((), ()))
    for b in range(3):
        one = lax.dot_general(left_ref[...], high_ref[b], dims, preferred_element_type=jnp.float32)
        two = lax.dot_general(left_ref[...], low_ref[b], dims, preferred_element_type=jnp.float32)
        cov_ref[b] = one[:96] + (one[96:] + two[:96] + two[96:])
    row_root = 1.0 / jnp.sqrt(norm + 1e-6)
    tiles = []
    for t in range(2):
        lanes = slice(128 * t, 128 * t + 128)
        columns = norm_ref[0:1, lanes]
        scale = row_root * (1.0 / jnp.sqrt(columns + 1e-6))
        cov = [[cov_ref[b, 32 * a : 32 * a + 32, lanes] for b in range(3)] for a in range(3)]
        aligned = polar_trace(cov, scale)
        tiles.append((norm + columns - 2.0 * aligned) * (1.0 / ATOMS))
    if out_ref.shape[1] == 128:
        out_ref[...] = tiles[0]
    else:
        prev, own, nxt = tiles[0][:, :64], tiles[0][:, 64:], tiles[1][:, :64]
        out_ref[...] = jnp.concatenate([prev, prev, own, own, nxt, nxt], axis=1)


def own_kernel(rows_ref, high_ref, low_ref, norm_ref, partner_ref, out_ref, message_ref, left_ref, cov_ref):
    fill_rows(rows_ref, high_ref, low_ref, norm_ref, out_ref, left_ref, cov_ref)
    message_ref[...] = jnp.concatenate([out_ref[:, :64], partner_ref[:, :64]], axis=1)


def partner_kernel(chip_ref, rows_ref, high_ref, low_ref, norm_ref, *refs, before):
    out_ref, left_ref, cov_ref = refs[-3:]
    here = (chip_ref[0] % PLANE == PLANE - 1) == before

    @pl.when(here)
    def _():
        fill_rows(rows_ref, high_ref, low_ref, norm_ref, out_ref, left_ref, cov_ref)

    @pl.when(jnp.logical_not(here))
    def _():
        out_ref[...] = jnp.zeros_like(out_ref)


def next_kernel(chip_ref, core_ref, tiles_ref, mine_ref, other_ref, out_ref):
    chip, core = chip_ref[0], core_ref[0]
    out_ref[...] = tiles_ref[...]

    @pl.when(chip % PLANE == PLANE - 1)
    def _():
        mine, other = mine_ref[...], other_ref[...]
        zero = core == 0
        pair = jnp.concatenate([jnp.where(zero, mine, other), jnp.where(zero, other, mine)], axis=0)
        pair = jnp.concatenate([pair, pair], axis=0)
        turned = jnp.transpose(pair)[:, :64]
        same = jnp.where(zero, turned[0:32], turned[32:64])
        cross = jnp.where(zero, turned[64:96], turned[96:128])
        first = (chip + 1) % CHIPS // (CHIPS // 2) == 0
        out_ref[:, 256:384] = jnp.concatenate(
            [jnp.where(first, same, cross), jnp.where(first, cross, same)], axis=1
        )


def final_kernel(chip_ref, tiles_ref, far_ref, out_ref):
    chip = chip_ref[0]
    out_ref[...] = tiles_ref[...]

    @pl.when(chip % PLANE == PLANE - 1)
    def _():
        prev, own = far_ref[:, :64], far_ref[:, 64:]
        far = jnp.concatenate([prev, prev, own, own], axis=1)
        out_ref[:, :256] = jnp.where(is_here(chip)[:, :256], tiles_ref[:, :256], far)


def is_here(chip):
    lane = lax.broadcasted_iota(jnp.int32, (32, 384), 1)
    return (chip + (CHIPS - 1) + lane // 128) % CHIPS // (CHIPS // 2) == lane // 64 % 2


def tiles_kernel(chip_ref, own_ref, far_ref, out_ref):
    out_ref[...] = jnp.where(is_here(chip_ref[0]), own_ref[...], far_ref[...])


def small_call(kernel, scalars, arrays, name):
    return pl.pallas_call(
        kernel,
        out_shape=TILES,
        in_specs=[pl.BlockSpec(memory_space=pltpu.SMEM)] * len(scalars) + [SPEC] * len(arrays),
        out_specs=SPEC,
        compiler_params=pltpu.CompilerParams(vmem_limit_bytes=2 << 20),
        name=name,
    )(*scalars, *arrays)


def prepare(core, *frames):
    spec = pl.BlockSpec(memory_space=pltpu.VMEM)
    wide = jax.ShapeDtypeStruct((3, 256, ATOMS), jnp.bfloat16)
    return pl.pallas_call(
        prepare_kernel,
        out_shape=(wide, wide, jax.ShapeDtypeStruct((8, 256), jnp.float32)),
        in_specs=[pl.BlockSpec(memory_space=pltpu.SMEM)] + [spec] * 6,
        out_specs=(spec, spec, spec),
        scratch_shapes=[pltpu.VMEM((256, 128), jnp.float32)],
        compiler_params=pltpu.CompilerParams(vmem_limit_bytes=24 << 20),
        name="prepare",
    )(core, *frames)


SPEC = pl.BlockSpec(memory_space=pltpu.VMEM)
SCRATCH = [pltpu.VMEM((192, ATOMS), jnp.bfloat16), pltpu.VMEM((3, 96, 256), jnp.float32)]
TILES = jax.ShapeDtypeStruct((32, 384), jnp.float32)
MESSAGE = jax.ShapeDtypeStruct((32, 128), jnp.float32)


def own_rows(rows, high, low, norm, partner):
    return pl.pallas_call(
        own_kernel,
        out_shape=(TILES, MESSAGE),
        in_specs=[SPEC] * 5,
        out_specs=(SPEC, SPEC),
        scratch_shapes=SCRATCH,
        compiler_params=pltpu.CompilerParams(vmem_limit_bytes=24 << 20),
        name="rows_of_own",
    )(rows, high, low, norm, partner)


def partner_rows(chip, before, *arrays):
    return pl.pallas_call(
        functools.partial(partner_kernel, before=before),
        out_shape=MESSAGE if before else TILES,
        in_specs=[pl.BlockSpec(memory_space=pltpu.SMEM)] + [SPEC] * len(arrays),
        out_specs=SPEC,
        scratch_shapes=SCRATCH,
        compiler_params=pltpu.CompilerParams(vmem_limit_bytes=24 << 20),
        name="rows_of_partner",
    )(chip, *arrays)


def on_device(frames):
    rep = lax.axis_index("rep")
    core = rep % 2
    chip = rep // 2 * (CHIPS // 2) + lax.axis_index("blk")
    always = chip < CHIPS
    chips = range(CHIPS)
    afters = [c for c in chips if c % PLANE == 0]
    befores = [c for c in chips if c % PLANE == PLANE - 1]
    not_after = [c for c in chips if c not in afters]
    not_before = [c for c in chips if c not in befores]
    half = CHIPS // 2
    raw = frames.transpose(1, 0, 2).reshape(96, ATOMS)

    prv = moved(raw, 1, 0)
    nxt = moved(raw, -1, 0, not_after)
    far = moved(raw, half, 0, not_before)
    far_before = moved(raw, half, 0, befores)

    def swap_near(prv, nxt):
        return moved(prv, 0, 1), moved(nxt, 0, 1, not_before)

    raw_other, then = lax.cond(always, lambda raw: (moved(raw, 0, 1), chip), lambda raw: (raw, chip), raw)
    prv_other, nxt_other = lax.cond(then < CHIPS, swap_near, lambda prv, nxt: (prv, nxt), prv, nxt)
    place = tuple(value.reshape(1).astype(jnp.int32) for value in (chip, core))
    columns = prepare(place[1], prv, prv_other, raw, raw_other, nxt, nxt_other)
    for_partner = partner_rows(place[0], False, far, *columns)
    returned = moved(for_partner, half, 0, not_before)
    own, message = own_rows(raw, *columns, for_partner)
    mine = moved(message, -1, 0, afters)
    other = moved(message, -1, 1, afters)
    for_partner_before = partner_rows(place[0], True, far_before, *columns, message)
    returned_before = moved(for_partner_before, half, 0, befores)
    tiles = small_call(tiles_kernel, place[:1], (own, returned), "tiles")
    tiles = small_call(next_kernel, place, (tiles, mine, other), "next_columns")
    return small_call(final_kernel, place[:1], (tiles, returned_before), "final")


def solution(mesh):
    return jax.shard_map(
        on_device,
        mesh=mesh,
        in_specs=(P(AXES, None, None),),
        out_specs=P(AXES, None),
        check_vma=False,
    )
```

```python
import functools

import jax
import jax.numpy as jnp
from jax import lax
from jax.experimental import pallas as pl
from jax.experimental.pallas import tpu as pltpu
from jax.sharding import PartitionSpec as P

ITERS = 8
ATOMS = 1024
AXES = ("blk", "rep")
CHIPS = 256
PLANE = 32


def device_of(chip, core):
    half, block = divmod(chip % CHIPS, CHIPS // 2)
    return block * 4 + half * 2 + core


def moved(value, chips, cores, senders=range(CHIPS)):
    pairs = [
        (device_of(chip, core), device_of(chip + chips, (core + cores) % 2))
        for chip in senders
        for core in range(2)
    ]
    return lax.ppermute(value, AXES, pairs)


def centred_of(raw):
    return raw - jnp.sum(raw, axis=1, keepdims=True) * (1.0 / ATOMS)


def split(value):
    high = value.astype(jnp.bfloat16)
    low = (value - high.astype(jnp.float32)).astype(jnp.bfloat16)
    return high, low


def prepare_kernel(core_ref, *refs):
    frames, (high_ref, low_ref, norm_ref, column_ref) = refs[:6], refs[6:]
    core = core_ref[0]
    column_ref[...] = jnp.zeros_like(column_ref)
    for n, ref in enumerate(frames):
        at = core if n % 2 == 0 else 1 - core
        start = pl.multiple_of(64 * (n // 2) + 32 * at, 32)
        norm = jnp.zeros((32, 1), jnp.float32)
        for b in range(3):
            centred = centred_of(ref[32 * b : 32 * b + 32, :])
            norm = norm + jnp.sum(centred * centred, axis=1, keepdims=True)
            high, low = split(centred)
            high_ref[b, pl.ds(start, 32), :] = high
            low_ref[b, pl.ds(start, 32), :] = low
        column_ref[pl.ds(start, 32), :] = jnp.broadcast_to(norm, (32, 128))
    for b in range(3):
        high_ref[b, 192:256, :] = jnp.zeros((64, ATOMS), jnp.bfloat16)
        low_ref[b, 192:256, :] = jnp.zeros((64, ATOMS), jnp.bfloat16)
    norm_ref[...] = jnp.transpose(column_ref[...])[0:8, :]


def polar_trace(cov, scale):
    x = [[cov[a][b] * scale for b in range(3)] for a in range(3)]
    for _ in range(ITERS):
        m = {}
        for p in range(3):
            for q in range(p, 3):
                g = x[0][p] * x[0][q] + x[1][p] * x[1][q] + x[2][p] * x[2][q]
                m[p, q] = m[q, p] = 1.5 - 0.5 * g if p == q else -0.5 * g
        x = [[x[a][0] * m[0, b] + x[a][1] * m[1, b] + x[a][2] * m[2, b] for b in range(3)] for a in range(3)]
    return sum(x[a][b] * cov[a][b] for a in range(3) for b in range(3))


def fill_rows(rows_ref, high_ref, low_ref, norm_ref, out_ref, left_ref, cov_ref):
    norm = jnp.zeros((32, 1), jnp.float32)
    for a in range(3):
        centred = centred_of(rows_ref[32 * a : 32 * a + 32, :])
        norm = norm + jnp.sum(centred * centred, axis=1, keepdims=True)
        high, low = split(centred)
        left_ref[32 * a : 32 * a + 32, :] = high
        left_ref[96 + 32 * a : 128 + 32 * a, :] = low
    dims = (((1,), (1,)), ((), ()))
    for b in range(3):
        one = lax.dot_general(left_ref[...], high_ref[b], dims, preferred_element_type=jnp.float32)
        two = lax.dot_general(left_ref[...], low_ref[b], dims, preferred_element_type=jnp.float32)
        cov_ref[b] = one[:96] + (one[96:] + two[:96] + two[96:])
    row_root = 1.0 / jnp.sqrt(norm + 1e-6)
    tiles = []
    for t in range(2):
        lanes = slice(128 * t, 128 * t + 128)
        columns = norm_ref[0:1, lanes]
        scale = row_root * (1.0 / jnp.sqrt(columns + 1e-6))
        cov = [[cov_ref[b, 32 * a : 32 * a + 32, lanes] for b in range(3)] for a in range(3)]
        aligned = polar_trace(cov, scale)
        tiles.append((norm + columns - 2.0 * aligned) * (1.0 / ATOMS))
    if out_ref.shape[1] == 128:
        out_ref[0:32, :] = tiles[0]
        if out_ref.shape[0] == 48:
            out_ref[32:48, :] = jnp.concatenate([tiles[1][:16, :64], tiles[1][16:, :64]], axis=1)
    else:
        out_ref[...] = doubled(tiles[0], tiles[1][:, :64])


def doubled(first, nxt):
    prev, own = first[:, :64], first[:, 64:]
    return jnp.concatenate([prev, prev, own, own, nxt, nxt], axis=1)


def is_late(chip):
    return jnp.logical_and(chip % PLANE == 0, jnp.logical_or(chip == 0, chip // PLANE >= 3))


def early_kernel(chip_ref, rows_ref, high_ref, low_ref, norm_ref, out_ref, left_ref, cov_ref):
    late = is_late(chip_ref[0])

    @pl.when(jnp.logical_not(late))
    def _():
        fill_rows(rows_ref, high_ref, low_ref, norm_ref, out_ref, left_ref, cov_ref)

    @pl.when(late)
    def _():
        out_ref[...] = jnp.zeros_like(out_ref)


def own_kernel(chip_ref, rows_ref, high_ref, low_ref, norm_ref, early_ref, partner_ref, out_ref, message_ref, left_ref, cov_ref):
    late = is_late(chip_ref[0])

    @pl.when(late)
    def _():
        fill_rows(rows_ref, high_ref, low_ref, norm_ref, out_ref, left_ref, cov_ref)

    @pl.when(jnp.logical_not(late))
    def _():
        out_ref[...] = early_ref[...]

    message_ref[...] = jnp.concatenate([out_ref[:, :64], partner_ref[0:32, :64]], axis=1)


def partner_kernel(chip_ref, rows_ref, high_ref, low_ref, norm_ref, *refs, before):
    out_ref, left_ref, cov_ref = refs[-3:]
    here = (chip_ref[0] % PLANE == PLANE - 1) == before

    @pl.when(here)
    def _():
        fill_rows(rows_ref, high_ref, low_ref, norm_ref, out_ref, left_ref, cov_ref)

    @pl.when(jnp.logical_not(here))
    def _():
        out_ref[...] = jnp.zeros_like(out_ref)


def next_kernel(chip_ref, core_ref, tiles_ref, mine_ref, other_ref, out_ref):
    chip, core = chip_ref[0], core_ref[0]
    out_ref[...] = tiles_ref[...]

    @pl.when(chip % PLANE == PLANE - 1)
    def _():
        mine, other = mine_ref[...], other_ref[...]
        zero = core == 0
        pair = jnp.concatenate([jnp.where(zero, mine, other), jnp.where(zero, other, mine)], axis=0)
        pair = jnp.concatenate([pair, pair], axis=0)
        turned = jnp.transpose(pair)[:, :64]
        same = jnp.where(zero, turned[0:32], turned[32:64])
        cross = jnp.where(zero, turned[64:96], turned[96:128])
        first = (chip + 1) % CHIPS // (CHIPS // 2) == 0
        out_ref[:, 256:384] = jnp.concatenate(
            [jnp.where(first, same, cross), jnp.where(first, cross, same)], axis=1
        )


def final_kernel(chip_ref, tiles_ref, far_ref, out_ref):
    chip = chip_ref[0]
    out_ref[...] = tiles_ref[...]

    @pl.when(chip % PLANE == PLANE - 1)
    def _():
        prev, own = far_ref[:, :64], far_ref[:, 64:]
        far = jnp.concatenate([prev, prev, own, own], axis=1)
        out_ref[:, :256] = jnp.where(is_here(chip)[:, :256], tiles_ref[:, :256], far)


def is_here(chip):
    lane = lax.broadcasted_iota(jnp.int32, (32, 384), 1)
    return (chip + (CHIPS - 1) + lane // 128) % CHIPS // (CHIPS // 2) == lane // 64 % 2


def tiles_kernel(chip_ref, own_ref, far_ref, out_ref):
    nxt = jnp.concatenate([far_ref[32:48, :64], far_ref[32:48, 64:]], axis=0)
    out_ref[...] = jnp.where(is_here(chip_ref[0]), own_ref[...], doubled(far_ref[0:32, :], nxt))


def small_call(kernel, scalars, arrays, name):
    return pl.pallas_call(
        kernel,
        out_shape=TILES,
        in_specs=[pl.BlockSpec(memory_space=pltpu.SMEM)] * len(scalars) + [SPEC] * len(arrays),
        out_specs=SPEC,
        compiler_params=pltpu.CompilerParams(vmem_limit_bytes=2 << 20),
        name=name,
    )(*scalars, *arrays)


def prepare(core, *frames):
    spec = pl.BlockSpec(memory_space=pltpu.VMEM)
    wide = jax.ShapeDtypeStruct((3, 256, ATOMS), jnp.bfloat16)
    return pl.pallas_call(
        prepare_kernel,
        out_shape=(wide, wide, jax.ShapeDtypeStruct((8, 256), jnp.float32)),
        in_specs=[pl.BlockSpec(memory_space=pltpu.SMEM)] + [spec] * 6,
        out_specs=(spec, spec, spec),
        scratch_shapes=[pltpu.VMEM((256, 128), jnp.float32)],
        compiler_params=pltpu.CompilerParams(vmem_limit_bytes=24 << 20),
        name="prepare",
    )(core, *frames)


SPEC = pl.BlockSpec(memory_space=pltpu.VMEM)
SCRATCH = [pltpu.VMEM((192, ATOMS), jnp.bfloat16), pltpu.VMEM((3, 96, 256), jnp.float32)]
TILES = jax.ShapeDtypeStruct((32, 384), jnp.float32)
MESSAGE = jax.ShapeDtypeStruct((32, 128), jnp.float32)
PACKED = jax.ShapeDtypeStruct((48, 128), jnp.float32)


def own_rows(chip, rows, high, low, norm, *more):
    return pl.pallas_call(
        own_kernel if more else early_kernel,
        out_shape=(TILES, MESSAGE) if more else TILES,
        in_specs=[pl.BlockSpec(memory_space=pltpu.SMEM)] + [SPEC] * (4 + len(more)),
        out_specs=(SPEC, SPEC) if more else SPEC,
        scratch_shapes=SCRATCH,
        compiler_params=pltpu.CompilerParams(vmem_limit_bytes=24 << 20),
        name="rows_of_own" if more else "early_rows_of_own",
    )(chip, rows, high, low, norm, *more)


def partner_rows(chip, before, *arrays):
    return pl.pallas_call(
        functools.partial(partner_kernel, before=before),
        out_shape=MESSAGE if before else PACKED,
        in_specs=[pl.BlockSpec(memory_space=pltpu.SMEM)] + [SPEC] * len(arrays),
        out_specs=SPEC,
        scratch_shapes=SCRATCH,
        compiler_params=pltpu.CompilerParams(vmem_limit_bytes=24 << 20),
        name="rows_of_partner",
    )(chip, *arrays)


def on_device(frames):
    rep = lax.axis_index("rep")
    core = rep % 2
    chip = rep // 2 * (CHIPS // 2) + lax.axis_index("blk")
    always = chip < CHIPS
    chips = range(CHIPS)
    afters = [c for c in chips if c % PLANE == 0]
    befores = [c for c in chips if c % PLANE == PLANE - 1]
    not_after = [c for c in chips if c not in afters]
    not_before = [c for c in chips if c not in befores]
    half = CHIPS // 2
    raw = frames.transpose(1, 0, 2).reshape(96, ATOMS)

    prv = moved(raw, 1, 0)
    nxt = moved(raw, -1, 0, not_after)
    far = moved(raw, half, 0, not_before)
    far_before = moved(raw, half, 0, befores)

    def swap_near(prv, nxt):
        return moved(prv, 0, 1), moved(nxt, 0, 1, not_before)

    raw_other, then = lax.cond(always, lambda raw: (moved(raw, 0, 1), chip), lambda raw: (raw, chip), raw)
    prv_other, nxt_other = lax.cond(then < CHIPS, swap_near, lambda prv, nxt: (prv, nxt), prv, nxt)
    place = tuple(value.reshape(1).astype(jnp.int32) for value in (chip, core))
    columns = prepare(place[1], prv, prv_other, raw, raw_other, nxt, nxt_other)
    early = own_rows(place[0], raw, *columns)
    for_partner = partner_rows(place[0], False, far, *columns, early)
    returned = moved(for_partner, half, 0, not_before)
    own, message = own_rows(place[0], raw, *columns, early, for_partner)
    mine = moved(message, -1, 0, afters)
    other = moved(message, -1, 1, afters)
    for_partner_before = partner_rows(place[0], True, far_before, *columns, message)
    returned_before = moved(for_partner_before, half, 0, befores)
    tiles = small_call(tiles_kernel, place[:1], (own, returned), "tiles")
    tiles = small_call(next_kernel, place, (tiles, mine, other), "next_columns")
    return small_call(final_kernel, place[:1], (tiles, returned_before), "final")


def solution(mesh):
    return jax.shard_map(
        on_device,
        mesh=mesh,
        in_specs=(P(AXES, None, None),),
        out_specs=P(AXES, None),
        check_vma=False,
    )
```

```python
import functools

import jax
import jax.numpy as jnp
from jax import lax
from jax.experimental import pallas as pl
from jax.experimental.pallas import tpu as pltpu
from jax.sharding import PartitionSpec as P

ITERS = 8
ATOMS = 1024
AXES = ("blk", "rep")
CHIPS = 256
PLANE = 32


def device_of(chip, core):
    half, block = divmod(chip % CHIPS, CHIPS // 2)
    return block * 4 + half * 2 + core


def moved(value, chips, cores, senders=range(CHIPS)):
    pairs = [
        (device_of(chip, core), device_of(chip + chips, (core + cores) % 2))
        for chip in senders
        for core in range(2)
    ]
    return lax.ppermute(value, AXES, pairs)


def stepped(value, steps):
    pairs = [(device_of(chip, core), device_of(chip + step, core)) for chip, step in steps for core in range(2)]
    return lax.ppermute(value, AXES, pairs)


def centred_of(raw):
    return raw - jnp.sum(raw, axis=1, keepdims=True) * (1.0 / ATOMS)


def split(value):
    high = value.astype(jnp.bfloat16)
    low = (value - high.astype(jnp.float32)).astype(jnp.bfloat16)
    return high, low


def prepare_kernel(chip_ref, core_ref, *refs):
    frames, (high_ref, low_ref, norm_ref, column_ref) = refs[:6], refs[6:]
    core, odd = core_ref[0], chip_ref[0] % 2
    column_ref[...] = jnp.zeros_like(column_ref)
    for n, ref in enumerate(frames):
        at = core if n % 2 == 0 else 1 - core
        group = (2 * odd, 1, 2 - 2 * odd)[n // 2]
        start = pl.multiple_of(64 * group + 32 * at, 32)
        norm = jnp.zeros((32, 1), jnp.float32)
        for b in range(3):
            centred = centred_of(ref[32 * b : 32 * b + 32, :])
            norm = norm + jnp.sum(centred * centred, axis=1, keepdims=True)
            high, low = split(centred)
            high_ref[b, pl.ds(start, 32), :] = high
            low_ref[b, pl.ds(start, 32), :] = low
        column_ref[pl.ds(start, 32), :] = jnp.broadcast_to(norm, (32, 128))
    for b in range(3):
        high_ref[b, 192:256, :] = jnp.zeros((64, ATOMS), jnp.bfloat16)
        low_ref[b, 192:256, :] = jnp.zeros((64, ATOMS), jnp.bfloat16)
    norm_ref[...] = jnp.transpose(column_ref[...])[0:8, :]


def polar_trace(cov, scale):
    x = [[cov[a][b] * scale for b in range(3)] for a in range(3)]
    for _ in range(ITERS):
        m = {}
        for p in range(3):
            for q in range(p, 3):
                g = x[0][p] * x[0][q] + x[1][p] * x[1][q] + x[2][p] * x[2][q]
                m[p, q] = m[q, p] = 1.5 - 0.5 * g if p == q else -0.5 * g
        x = [[x[a][0] * m[0, b] + x[a][1] * m[1, b] + x[a][2] * m[2, b] for b in range(3)] for a in range(3)]
    return sum(x[a][b] * cov[a][b] for a in range(3) for b in range(3))


def fill_rows(rows_ref, high_ref, low_ref, norm_ref, out_ref, left_ref, cov_ref):
    norm = jnp.zeros((32, 1), jnp.float32)
    for a in range(3):
        centred = centred_of(rows_ref[32 * a : 32 * a + 32, :])
        norm = norm + jnp.sum(centred * centred, axis=1, keepdims=True)
        high, low = split(centred)
        left_ref[32 * a : 32 * a + 32, :] = high
        left_ref[96 + 32 * a : 128 + 32 * a, :] = low
    dims = (((1,), (1,)), ((), ()))
    for b in range(3):
        one = lax.dot_general(left_ref[...], high_ref[b], dims, preferred_element_type=jnp.float32)
        two = lax.dot_general(left_ref[...], low_ref[b], dims, preferred_element_type=jnp.float32)
        cov_ref[b] = one[:96] + (one[96:] + two[:96] + two[96:])
    row_root = 1.0 / jnp.sqrt(norm + 1e-6)
    tiles = []
    for t in range(2):
        lanes = slice(128 * t, 128 * t + 128)
        columns = norm_ref[0:1, lanes]
        scale = row_root * (1.0 / jnp.sqrt(columns + 1e-6))
        cov = [[cov_ref[b, 32 * a : 32 * a + 32, lanes] for b in range(3)] for a in range(3)]
        aligned = polar_trace(cov, scale)
        tiles.append((norm + columns - 2.0 * aligned) * (1.0 / ATOMS))
    if out_ref.shape[1] == 128:
        out_ref[0:32, :] = tiles[0]
        if out_ref.shape[0] == 48:
            out_ref[32:48, :] = jnp.concatenate([tiles[1][:16, :64], tiles[1][16:, :64]], axis=1)
    else:
        out_ref[...] = doubled(tiles[0], tiles[1][:, :64])


def doubled(first, nxt):
    prev, own = first[:, :64], first[:, 64:]
    return jnp.concatenate([prev, prev, own, own, nxt, nxt], axis=1)


def is_late(chip):
    return jnp.logical_and(chip % PLANE == 0, jnp.logical_or(chip == 0, chip // PLANE >= 3))


def early_kernel(chip_ref, rows_ref, high_ref, low_ref, norm_ref, out_ref, left_ref, cov_ref):
    late = is_late(chip_ref[0])

    @pl.when(jnp.logical_not(late))
    def _():
        fill_rows(rows_ref, high_ref, low_ref, norm_ref, out_ref, left_ref, cov_ref)

    @pl.when(late)
    def _():
        out_ref[...] = jnp.zeros_like(out_ref)


def own_kernel(chip_ref, rows_ref, high_ref, low_ref, norm_ref, early_ref, partner_ref, out_ref, message_ref, left_ref, cov_ref):
    late = is_late(chip_ref[0])

    @pl.when(late)
    def _():
        fill_rows(rows_ref, high_ref, low_ref, norm_ref, out_ref, left_ref, cov_ref)

    @pl.when(jnp.logical_not(late))
    def _():
        out_ref[...] = early_ref[...]

    message_ref[...] = jnp.concatenate([out_ref[:, :64], partner_ref[0:32, :64]], axis=1)


def partner_kernel(chip_ref, rows_ref, high_ref, low_ref, norm_ref, *refs, before):
    out_ref, left_ref, cov_ref = refs[-3:]
    here = (chip_ref[0] % PLANE == PLANE - 1) == before

    @pl.when(here)
    def _():
        fill_rows(rows_ref, high_ref, low_ref, norm_ref, out_ref, left_ref, cov_ref)

    @pl.when(jnp.logical_not(here))
    def _():
        out_ref[...] = jnp.zeros_like(out_ref)


def next_kernel(chip_ref, core_ref, tiles_ref, mine_ref, other_ref, out_ref):
    chip, core = chip_ref[0], core_ref[0]
    out_ref[...] = tiles_ref[...]

    @pl.when(chip % PLANE == PLANE - 1)
    def _():
        mine, other = mine_ref[...], other_ref[...]
        zero = core == 0
        pair = jnp.concatenate([jnp.where(zero, mine, other), jnp.where(zero, other, mine)], axis=0)
        pair = jnp.concatenate([pair, pair], axis=0)
        turned = jnp.transpose(pair)[:, :64]
        same = jnp.where(zero, turned[0:32], turned[32:64])
        cross = jnp.where(zero, turned[64:96], turned[96:128])
        first = (chip + 1) % CHIPS // (CHIPS // 2) == 0
        out_ref[:, 256:384] = jnp.concatenate(
            [jnp.where(first, same, cross), jnp.where(first, cross, same)], axis=1
        )


def final_kernel(chip_ref, tiles_ref, far_ref, out_ref):
    chip = chip_ref[0]
    out_ref[...] = tiles_ref[...]

    @pl.when(chip % PLANE == PLANE - 1)
    def _():
        prev, own = far_ref[:, :64], far_ref[:, 64:]
        far = jnp.concatenate([prev, prev, own, own], axis=1)
        out_ref[:, :256] = jnp.where(is_here(chip)[:, :256], tiles_ref[:, :256], far)


def is_here(chip):
    lane = lax.broadcasted_iota(jnp.int32, (32, 384), 1)
    return (chip + (CHIPS - 1) + lane // 128) % CHIPS // (CHIPS // 2) == lane // 64 % 2


def tiles_kernel(chip_ref, own_ref, far_ref, out_ref):
    nxt = jnp.concatenate([far_ref[32:48, :64], far_ref[32:48, 64:]], axis=0)
    out_ref[...] = jnp.where(is_here(chip_ref[0]), own_ref[...], doubled(far_ref[0:32, :], nxt))


def small_call(kernel, scalars, arrays, name):
    return pl.pallas_call(
        kernel,
        out_shape=TILES,
        in_specs=[pl.BlockSpec(memory_space=pltpu.SMEM)] * len(scalars) + [SPEC] * len(arrays),
        out_specs=SPEC,
        compiler_params=pltpu.CompilerParams(vmem_limit_bytes=2 << 20),
        name=name,
    )(*scalars, *arrays)


def prepare(chip, core, *frames):
    spec = pl.BlockSpec(memory_space=pltpu.VMEM)
    wide = jax.ShapeDtypeStruct((3, 256, ATOMS), jnp.bfloat16)
    return pl.pallas_call(
        prepare_kernel,
        out_shape=(wide, wide, jax.ShapeDtypeStruct((8, 256), jnp.float32)),
        in_specs=[pl.BlockSpec(memory_space=pltpu.SMEM)] * 2 + [spec] * 6,
        out_specs=(spec, spec, spec),
        scratch_shapes=[pltpu.VMEM((256, 128), jnp.float32)],
        compiler_params=pltpu.CompilerParams(vmem_limit_bytes=24 << 20),
        name="prepare",
    )(chip, core, *frames)


SPEC = pl.BlockSpec(memory_space=pltpu.VMEM)
SCRATCH = [pltpu.VMEM((192, ATOMS), jnp.bfloat16), pltpu.VMEM((3, 96, 256), jnp.float32)]
TILES = jax.ShapeDtypeStruct((32, 384), jnp.float32)
MESSAGE = jax.ShapeDtypeStruct((32, 128), jnp.float32)
PACKED = jax.ShapeDtypeStruct((48, 128), jnp.float32)


def own_rows(chip, rows, high, low, norm, *more):
    return pl.pallas_call(
        own_kernel if more else early_kernel,
        out_shape=(TILES, MESSAGE) if more else TILES,
        in_specs=[pl.BlockSpec(memory_space=pltpu.SMEM)] + [SPEC] * (4 + len(more)),
        out_specs=(SPEC, SPEC) if more else SPEC,
        scratch_shapes=SCRATCH,
        compiler_params=pltpu.CompilerParams(vmem_limit_bytes=24 << 20),
        name="rows_of_own" if more else "early_rows_of_own",
    )(chip, rows, high, low, norm, *more)


def partner_rows(chip, before, *arrays):
    return pl.pallas_call(
        functools.partial(partner_kernel, before=before),
        out_shape=MESSAGE if before else PACKED,
        in_specs=[pl.BlockSpec(memory_space=pltpu.SMEM)] + [SPEC] * len(arrays),
        out_specs=SPEC,
        scratch_shapes=SCRATCH,
        compiler_params=pltpu.CompilerParams(vmem_limit_bytes=24 << 20),
        name="rows_of_partner",
    )(chip, *arrays)


def on_device(frames):
    rep = lax.axis_index("rep")
    core = rep % 2
    chip = rep // 2 * (CHIPS // 2) + lax.axis_index("blk")
    always = chip < CHIPS
    chips = range(CHIPS)
    afters = [c for c in chips if c % PLANE == 0]
    befores = [c for c in chips if c % PLANE == PLANE - 1]
    not_after = [c for c in chips if c not in afters]
    not_before = [c for c in chips if c not in befores]
    half = CHIPS // 2
    raw = frames.transpose(1, 0, 2).reshape(96, ATOMS)

    first = [(c, 1 if c % 2 else -1) for c in chips if c % PLANE]
    second = [(c, -1 if c % 2 else 1) for c in chips]
    one = stepped(raw, first)
    two = stepped(raw, second)
    far = moved(raw, half, 0, not_before)
    far_before = moved(raw, half, 0, befores)

    def swap_near(one, two):
        return moved(one, 0, 1, not_before), moved(two, 0, 1)

    raw_other, then = lax.cond(always, lambda raw: (moved(raw, 0, 1), chip), lambda raw: (raw, chip), raw)
    one_other, two_other = lax.cond(then < CHIPS, swap_near, lambda one, two: (one, two), one, two)
    place = tuple(value.reshape(1).astype(jnp.int32) for value in (chip, core))
    columns = prepare(*place, one, one_other, raw, raw_other, two, two_other)
    early = own_rows(place[0], raw, *columns)
    for_partner = partner_rows(place[0], False, far, *columns, early)
    returned = moved(for_partner, half, 0, not_before)
    own, message = own_rows(place[0], raw, *columns, early, for_partner)
    mine = moved(message, -1, 0, afters)
    other = moved(message, -1, 1, afters)
    for_partner_before = partner_rows(place[0], True, far_before, *columns, message)
    returned_before = moved(for_partner_before, half, 0, befores)
    tiles = small_call(tiles_kernel, place[:1], (own, returned), "tiles")
    tiles = small_call(next_kernel, place, (tiles, mine, other), "next_columns")
    return small_call(final_kernel, place[:1], (tiles, returned_before), "final")


def solution(mesh):
    return jax.shard_map(
        on_device,
        mesh=mesh,
        in_specs=(P(AXES, None, None),),
        out_specs=P(AXES, None),
        check_vma=False,
    )
```

```python
import functools

import jax
import jax.numpy as jnp
from jax import lax
from jax.experimental import pallas as pl
from jax.experimental.pallas import tpu as pltpu
from jax.sharding import PartitionSpec as P

ITERS = 8
ATOMS = 1024
AXES = ("blk", "rep")
CHIPS = 256
PLANE = 32


def device_of(chip, core):
    half, block = divmod(chip % CHIPS, CHIPS // 2)
    return block * 4 + half * 2 + core


def moved(value, chips, cores, senders=range(CHIPS)):
    pairs = [
        (device_of(chip, core), device_of(chip + chips, (core + cores) % 2))
        for chip in senders
        for core in range(2)
    ]
    return lax.ppermute(value, AXES, pairs)


def stepped(value, steps):
    pairs = [(device_of(chip, core), device_of(chip + step, core)) for chip, step in steps for core in range(2)]
    return lax.ppermute(value, AXES, pairs)


def centred_of(raw):
    return raw - jnp.sum(raw, axis=1, keepdims=True) * (1.0 / ATOMS)


def split(value):
    high = value.astype(jnp.bfloat16)
    low = (value - high.astype(jnp.float32)).astype(jnp.bfloat16)
    return high, low


def prepare_kernel(chip_ref, core_ref, *refs):
    frames, (high_ref, low_ref, norm_ref, column_ref) = refs[:6], refs[6:]
    core, odd = core_ref[0], chip_ref[0] % 2
    column_ref[...] = jnp.zeros_like(column_ref)
    for n, ref in enumerate(frames):
        at = core if n % 2 == 0 else 1 - core
        group = (2 * odd, 1, 2 - 2 * odd)[n // 2]
        start = pl.multiple_of(64 * group + 32 * at, 32)
        norm = jnp.zeros((32, 1), jnp.float32)
        for b in range(3):
            centred = centred_of(ref[32 * b : 32 * b + 32, :])
            norm = norm + jnp.sum(centred * centred, axis=1, keepdims=True)
            high, low = split(centred)
            high_ref[b, pl.ds(start, 32), :] = high
            low_ref[b, pl.ds(start, 32), :] = low
        column_ref[pl.ds(start, 32), :] = jnp.broadcast_to(norm, (32, 128))
    for b in range(3):
        high_ref[b, 192:256, :] = jnp.zeros((64, ATOMS), jnp.bfloat16)
        low_ref[b, 192:256, :] = jnp.zeros((64, ATOMS), jnp.bfloat16)
    norm_ref[...] = jnp.transpose(column_ref[...])[0:8, :]


def polar_trace(cov, scale):
    x = [[cov[a][b] * scale for b in range(3)] for a in range(3)]
    for _ in range(ITERS):
        m = {}
        for p in range(3):
            for q in range(p, 3):
                g = x[0][p] * x[0][q] + x[1][p] * x[1][q] + x[2][p] * x[2][q]
                m[p, q] = m[q, p] = 1.5 - 0.5 * g if p == q else -0.5 * g
        x = [[x[a][0] * m[0, b] + x[a][1] * m[1, b] + x[a][2] * m[2, b] for b in range(3)] for a in range(3)]
    return sum(x[a][b] * cov[a][b] for a in range(3) for b in range(3))


def fill_rows(rows_ref, high_ref, low_ref, norm_ref, out_ref, left_ref, cov_ref):
    norm = jnp.zeros((32, 1), jnp.float32)
    for a in range(3):
        centred = centred_of(rows_ref[32 * a : 32 * a + 32, :])
        norm = norm + jnp.sum(centred * centred, axis=1, keepdims=True)
        high, low = split(centred)
        left_ref[32 * a : 32 * a + 32, :] = high
        left_ref[96 + 32 * a : 128 + 32 * a, :] = low
    dims = (((1,), (1,)), ((), ()))
    for b in range(3):
        one = lax.dot_general(left_ref[...], high_ref[b], dims, preferred_element_type=jnp.float32)
        two = lax.dot_general(left_ref[...], low_ref[b], dims, preferred_element_type=jnp.float32)
        cov_ref[b] = one[:96] + (one[96:] + two[:96] + two[96:])
    row_root = 1.0 / jnp.sqrt(norm + 1e-6)
    tiles = []
    for t in range(2):
        lanes = slice(128 * t, 128 * t + 128)
        columns = norm_ref[0:1, lanes]
        scale = row_root * (1.0 / jnp.sqrt(columns + 1e-6))
        cov = [[cov_ref[b, 32 * a : 32 * a + 32, lanes] for b in range(3)] for a in range(3)]
        aligned = polar_trace(cov, scale)
        tiles.append((norm + columns - 2.0 * aligned) * (1.0 / ATOMS))
    if out_ref.shape[1] == 128:
        out_ref[0:32, :] = tiles[0]
        if out_ref.shape[0] == 48:
            out_ref[32:48, :] = jnp.concatenate([tiles[1][:16, :64], tiles[1][16:, :64]], axis=1)
    else:
        out_ref[...] = doubled(tiles[0], tiles[1][:, :64])


def doubled(first, nxt):
    prev, own = first[:, :64], first[:, 64:]
    return jnp.concatenate([prev, prev, own, own, nxt, nxt], axis=1)


def is_late(chip):
    return jnp.logical_and(chip % PLANE == 0, jnp.logical_or(chip == 0, chip // PLANE >= 3))


def early_kernel(chip_ref, rows_ref, high_ref, low_ref, norm_ref, out_ref, left_ref, cov_ref):
    late = is_late(chip_ref[0])

    @pl.when(jnp.logical_not(late))
    def _():
        fill_rows(rows_ref, high_ref, low_ref, norm_ref, out_ref, left_ref, cov_ref)

    @pl.when(late)
    def _():
        out_ref[...] = jnp.zeros_like(out_ref)


def own_kernel(chip_ref, rows_ref, high_ref, low_ref, norm_ref, early_ref, partner_ref, out_ref, message_ref, left_ref, cov_ref):
    late = is_late(chip_ref[0])

    @pl.when(late)
    def _():
        fill_rows(rows_ref, high_ref, low_ref, norm_ref, out_ref, left_ref, cov_ref)

    @pl.when(jnp.logical_not(late))
    def _():
        out_ref[...] = early_ref[...]

    message_ref[...] = jnp.concatenate([out_ref[:, :64], partner_ref[0:32, :64]], axis=1)


def partner_kernel(chip_ref, rows_ref, high_ref, low_ref, norm_ref, *refs, before):
    out_ref, left_ref, cov_ref = refs[-3:]
    here = (chip_ref[0] % PLANE == PLANE - 1) == before

    @pl.when(here)
    def _():
        fill_rows(rows_ref, high_ref, low_ref, norm_ref, out_ref, left_ref, cov_ref)

    @pl.when(jnp.logical_not(here))
    def _():
        out_ref[...] = jnp.zeros_like(out_ref)


def next_kernel(chip_ref, core_ref, tiles_ref, mine_ref, other_ref, out_ref):
    chip, core = chip_ref[0], core_ref[0]
    out_ref[...] = tiles_ref[...]

    @pl.when(chip % PLANE == PLANE - 1)
    def _():
        mine, other = mine_ref[...], other_ref[...]
        zero = core == 0
        pair = jnp.concatenate([jnp.where(zero, mine, other), jnp.where(zero, other, mine)], axis=0)
        pair = jnp.concatenate([pair, pair], axis=0)
        turned = jnp.transpose(pair)[:, :64]
        same = jnp.where(zero, turned[0:32], turned[32:64])
        cross = jnp.where(zero, turned[64:96], turned[96:128])
        first = (chip + 1) % CHIPS // (CHIPS // 2) == 0
        out_ref[:, 256:384] = jnp.concatenate(
            [jnp.where(first, same, cross), jnp.where(first, cross, same)], axis=1
        )


def final_kernel(chip_ref, tiles_ref, far_ref, out_ref):
    chip = chip_ref[0]
    out_ref[...] = tiles_ref[...]

    @pl.when(chip % PLANE == PLANE - 1)
    def _():
        prev, own = far_ref[:, :64], far_ref[:, 64:]
        far = jnp.concatenate([prev, prev, own, own], axis=1)
        out_ref[:, :256] = jnp.where(is_here(chip)[:, :256], tiles_ref[:, :256], far)


def is_here(chip):
    lane = lax.broadcasted_iota(jnp.int32, (32, 384), 1)
    return (chip + (CHIPS - 1) + lane // 128) % CHIPS // (CHIPS // 2) == lane // 64 % 2


def tiles_kernel(chip_ref, own_ref, far_ref, out_ref):
    nxt = jnp.concatenate([far_ref[32:48, :64], far_ref[32:48, 64:]], axis=0)
    out_ref[...] = jnp.where(is_here(chip_ref[0]), own_ref[...], doubled(far_ref[0:32, :], nxt))


def small_call(kernel, scalars, arrays, name):
    return pl.pallas_call(
        kernel,
        out_shape=TILES,
        in_specs=[pl.BlockSpec(memory_space=pltpu.SMEM)] * len(scalars) + [SPEC] * len(arrays),
        out_specs=SPEC,
        compiler_params=pltpu.CompilerParams(vmem_limit_bytes=2 << 20),
        name=name,
    )(*scalars, *arrays)


def prepare(chip, core, *frames):
    spec = pl.BlockSpec(memory_space=pltpu.VMEM)
    wide = jax.ShapeDtypeStruct((3, 256, ATOMS), jnp.bfloat16)
    return pl.pallas_call(
        prepare_kernel,
        out_shape=(wide, wide, jax.ShapeDtypeStruct((8, 256), jnp.float32)),
        in_specs=[pl.BlockSpec(memory_space=pltpu.SMEM)] * 2 + [spec] * 6,
        out_specs=(spec, spec, spec),
        scratch_shapes=[pltpu.VMEM((256, 128), jnp.float32)],
        compiler_params=pltpu.CompilerParams(vmem_limit_bytes=24 << 20),
        name="prepare",
    )(chip, core, *frames)


SPEC = pl.BlockSpec(memory_space=pltpu.VMEM)
SCRATCH = [pltpu.VMEM((192, ATOMS), jnp.bfloat16), pltpu.VMEM((3, 96, 256), jnp.float32)]
TILES = jax.ShapeDtypeStruct((32, 384), jnp.float32)
MESSAGE = jax.ShapeDtypeStruct((32, 128), jnp.float32)
PACKED = jax.ShapeDtypeStruct((48, 128), jnp.float32)


def own_rows(chip, rows, high, low, norm, *more):
    return pl.pallas_call(
        own_kernel if more else early_kernel,
        out_shape=(TILES, MESSAGE) if more else TILES,
        in_specs=[pl.BlockSpec(memory_space=pltpu.SMEM)] + [SPEC] * (4 + len(more)),
        out_specs=(SPEC, SPEC) if more else SPEC,
        scratch_shapes=SCRATCH,
        compiler_params=pltpu.CompilerParams(vmem_limit_bytes=24 << 20),
        name="rows_of_own" if more else "early_rows_of_own",
    )(chip, rows, high, low, norm, *more)


def partner_rows(chip, before, *arrays):
    return pl.pallas_call(
        functools.partial(partner_kernel, before=before),
        out_shape=MESSAGE if before else PACKED,
        in_specs=[pl.BlockSpec(memory_space=pltpu.SMEM)] + [SPEC] * len(arrays),
        out_specs=SPEC,
        scratch_shapes=SCRATCH,
        compiler_params=pltpu.CompilerParams(vmem_limit_bytes=24 << 20),
        name="rows_of_partner",
    )(chip, *arrays)


def on_device(frames):
    rep = lax.axis_index("rep")
    core = rep % 2
    chip = rep // 2 * (CHIPS // 2) + lax.axis_index("blk")
    always = chip < CHIPS
    chips = range(CHIPS)
    afters = [c for c in chips if c % PLANE == 0]
    befores = [c for c in chips if c % PLANE == PLANE - 1]
    not_after = [c for c in chips if c not in afters]
    not_before = [c for c in chips if c not in befores]
    half = CHIPS // 2
    raw = frames.transpose(1, 0, 2).reshape(96, ATOMS)

    first = [(c, 1 if c % 2 else -1) for c in chips if c % PLANE]
    second = [(c, -1 if c % 2 else 1) for c in chips]
    one = stepped(raw, first)
    two = stepped(raw, second)
    far = moved(raw, half, 0, not_before)
    far_before = moved(raw, half, 0, befores)

    def swap_near(one, two, scale):
        return moved(one, 0, 1, not_before) * scale, moved(two, 0, 1) * scale

    scale = always.astype(jnp.float32)
    raw_other, then = lax.cond(
        always, lambda raw, scale: (moved(raw, 0, 1) * scale, chip), lambda raw, _: (raw, chip), raw, scale
    )
    one_other, two_other = lax.cond(then < CHIPS, swap_near, lambda one, two, _: (one, two), one, two, scale)
    place = tuple(value.reshape(1).astype(jnp.int32) for value in (chip, core))
    columns = prepare(*place, one, one_other, raw, raw_other, two, two_other)
    early = own_rows(place[0], raw, *columns)
    for_partner = partner_rows(place[0], False, far, *columns, early)
    returned = moved(for_partner, half, 0, not_before)
    own, message = own_rows(place[0], raw, *columns, early, for_partner)
    mine = moved(message, -1, 0, afters)
    other = moved(message, -1, 1, afters)
    for_partner_before = partner_rows(place[0], True, far_before, *columns, message)
    returned_before = moved(for_partner_before, half, 0, befores)
    tiles = small_call(tiles_kernel, place[:1], (own, returned), "tiles")
    tiles = small_call(next_kernel, place, (tiles, mine, other), "next_columns")
    return small_call(final_kernel, place[:1], (tiles, returned_before), "final")


def solution(mesh):
    return jax.shard_map(
        on_device,
        mesh=mesh,
        in_specs=(P(AXES, None, None),),
        out_specs=P(AXES, None),
        check_vma=False,
    )
```

```python
import functools

import jax
import jax.numpy as jnp
from jax import lax
from jax.experimental import pallas as pl
from jax.experimental.pallas import tpu as pltpu
from jax.sharding import PartitionSpec as P

ITERS = 8
ATOMS = 1024
AXES = ("blk", "rep")
CHIPS = 256
PLANE = 32


def device_of(chip, core):
    half, block = divmod(chip % CHIPS, CHIPS // 2)
    return block * 4 + half * 2 + core


def moved(value, chips, cores, senders=range(CHIPS)):
    pairs = [
        (device_of(chip, core), device_of(chip + chips, (core + cores) % 2))
        for chip in senders
        for core in range(2)
    ]
    return lax.ppermute(value, AXES, pairs)


def stepped(value, steps):
    pairs = [(device_of(chip, core), device_of(chip + step, core)) for chip, step in steps for core in range(2)]
    return lax.ppermute(value, AXES, pairs)


def centred_of(raw):
    return raw - jnp.sum(raw, axis=1, keepdims=True) * (1.0 / ATOMS)


def split(value):
    high = value.astype(jnp.bfloat16)
    low = (value - high.astype(jnp.float32)).astype(jnp.bfloat16)
    return high, low


def prepare_kernel(chip_ref, core_ref, *refs):
    frames, (high_ref, low_ref, norm_ref, column_ref) = refs[:6], refs[6:]
    core, odd = core_ref[0], chip_ref[0] % 2
    column_ref[...] = jnp.zeros_like(column_ref)
    for n, ref in enumerate(frames):
        at = core if n % 2 == 0 else 1 - core
        group = (2 * odd, 1, 2 - 2 * odd)[n // 2]
        start = pl.multiple_of(64 * group + 32 * at, 32)
        norm = jnp.zeros((32, 1), jnp.float32)
        for b in range(3):
            centred = centred_of(ref[32 * b : 32 * b + 32, :])
            norm = norm + jnp.sum(centred * centred, axis=1, keepdims=True)
            high, low = split(centred)
            high_ref[b, pl.ds(start, 32), :] = high
            low_ref[b, pl.ds(start, 32), :] = low
        column_ref[pl.ds(start, 32), :] = jnp.broadcast_to(norm, (32, 128))
    norm_ref[...] = jnp.transpose(column_ref[...])[0:8, :]


def polar_trace(cov, scale):
    x = [[cov[a][b] * scale for b in range(3)] for a in range(3)]
    for _ in range(ITERS):
        m = {}
        for p in range(3):
            for q in range(p, 3):
                g = x[0][p] * x[0][q] + x[1][p] * x[1][q] + x[2][p] * x[2][q]
                m[p, q] = m[q, p] = 1.5 - 0.5 * g if p == q else -0.5 * g
        x = [[x[a][0] * m[0, b] + x[a][1] * m[1, b] + x[a][2] * m[2, b] for b in range(3)] for a in range(3)]
    return sum(x[a][b] * cov[a][b] for a in range(3) for b in range(3))


def folded(value):
    return jnp.concatenate([value[:16], value[16:]], axis=1)


def fill_rows(rows_ref, high_ref, low_ref, norm_ref, out_ref, left_ref, cov_ref):
    norm = jnp.zeros((32, 1), jnp.float32)
    for a in range(3):
        centred = centred_of(rows_ref[32 * a : 32 * a + 32, :])
        norm = norm + jnp.sum(centred * centred, axis=1, keepdims=True)
        high, low = split(centred)
        left_ref[32 * a : 32 * a + 32, :] = high
        left_ref[96 + 32 * a : 128 + 32 * a, :] = low
    dims = (((1,), (1,)), ((), ()))
    used = 128 if out_ref.shape == (32, 128) else 192
    for b in range(3):
        one = lax.dot_general(left_ref[...], high_ref[b, :used], dims, preferred_element_type=jnp.float32)
        two = lax.dot_general(left_ref[...], low_ref[b, :used], dims, preferred_element_type=jnp.float32)
        cov_ref[b, :, :used] = one[:96] + (one[96:] + two[:96] + two[96:])

    def tile(lanes, norm, columns, shaped=lambda value: value):
        scale = (1.0 / jnp.sqrt(norm + 1e-6)) * (1.0 / jnp.sqrt(columns + 1e-6))
        cov = [[shaped(cov_ref[b, 32 * a : 32 * a + 32, lanes]) for b in range(3)] for a in range(3)]
        return (norm + columns - 2.0 * polar_trace(cov, scale)) * (1.0 / ATOMS)

    first = tile(slice(0, 128), norm, norm_ref[0:1, :128])
    if used == 128:
        out_ref[...] = first
        return
    columns = norm_ref[0:1, 128:192]
    second = tile(
        slice(128, 192),
        folded(jnp.broadcast_to(norm, (32, 64))),
        jnp.concatenate([columns, columns], axis=1),
        folded,
    )
    if out_ref.shape[1] == 128:
        out_ref[0:32, :] = first
        out_ref[32:48, :] = second
    else:
        out_ref[...] = doubled(first, jnp.concatenate([second[:, :64], second[:, 64:]], axis=0))


def doubled(first, nxt):
    prev, own = first[:, :64], first[:, 64:]
    return jnp.concatenate([prev, prev, own, own, nxt, nxt], axis=1)


def is_late(chip):
    return jnp.logical_and(chip % PLANE == 0, jnp.logical_or(chip == 0, chip // PLANE >= 3))


def early_kernel(chip_ref, rows_ref, high_ref, low_ref, norm_ref, out_ref, left_ref, cov_ref):
    late = is_late(chip_ref[0])

    @pl.when(jnp.logical_not(late))
    def _():
        fill_rows(rows_ref, high_ref, low_ref, norm_ref, out_ref, left_ref, cov_ref)

    @pl.when(late)
    def _():
        out_ref[...] = jnp.zeros_like(out_ref)


def own_kernel(chip_ref, rows_ref, high_ref, low_ref, norm_ref, early_ref, partner_ref, out_ref, message_ref, left_ref, cov_ref):
    late = is_late(chip_ref[0])

    @pl.when(late)
    def _():
        fill_rows(rows_ref, high_ref, low_ref, norm_ref, out_ref, left_ref, cov_ref)

    @pl.when(jnp.logical_not(late))
    def _():
        out_ref[...] = early_ref[...]

    message_ref[...] = jnp.concatenate([out_ref[:, :64], partner_ref[0:32, :64]], axis=1)


def partner_kernel(chip_ref, rows_ref, high_ref, low_ref, norm_ref, *refs, before):
    out_ref, left_ref, cov_ref = refs[-3:]
    here = (chip_ref[0] % PLANE == PLANE - 1) == before

    @pl.when(here)
    def _():
        fill_rows(rows_ref, high_ref, low_ref, norm_ref, out_ref, left_ref, cov_ref)

    @pl.when(jnp.logical_not(here))
    def _():
        out_ref[...] = jnp.zeros_like(out_ref)


def next_kernel(chip_ref, core_ref, tiles_ref, mine_ref, other_ref, out_ref):
    chip, core = chip_ref[0], core_ref[0]
    out_ref[...] = tiles_ref[...]

    @pl.when(chip % PLANE == PLANE - 1)
    def _():
        mine, other = mine_ref[...], other_ref[...]
        zero = core == 0
        pair = jnp.concatenate([jnp.where(zero, mine, other), jnp.where(zero, other, mine)], axis=0)
        pair = jnp.concatenate([pair, pair], axis=0)
        turned = jnp.transpose(pair)[:, :64]
        same = jnp.where(zero, turned[0:32], turned[32:64])
        cross = jnp.where(zero, turned[64:96], turned[96:128])
        first = (chip + 1) % CHIPS // (CHIPS // 2) == 0
        out_ref[:, 256:384] = jnp.concatenate(
            [jnp.where(first, same, cross), jnp.where(first, cross, same)], axis=1
        )


def final_kernel(chip_ref, tiles_ref, far_ref, out_ref):
    chip = chip_ref[0]
    out_ref[...] = tiles_ref[...]

    @pl.when(chip % PLANE == PLANE - 1)
    def _():
        prev, own = far_ref[:, :64], far_ref[:, 64:]
        far = jnp.concatenate([prev, prev, own, own], axis=1)
        out_ref[:, :256] = jnp.where(is_here(chip)[:, :256], tiles_ref[:, :256], far)


def is_here(chip):
    lane = lax.broadcasted_iota(jnp.int32, (32, 384), 1)
    return (chip + (CHIPS - 1) + lane // 128) % CHIPS // (CHIPS // 2) == lane // 64 % 2


def tiles_kernel(chip_ref, own_ref, far_ref, out_ref):
    nxt = jnp.concatenate([far_ref[32:48, :64], far_ref[32:48, 64:]], axis=0)
    out_ref[...] = jnp.where(is_here(chip_ref[0]), own_ref[...], doubled(far_ref[0:32, :], nxt))


def small_call(kernel, scalars, arrays, name):
    return pl.pallas_call(
        kernel,
        out_shape=TILES,
        in_specs=[pl.BlockSpec(memory_space=pltpu.SMEM)] * len(scalars) + [SPEC] * len(arrays),
        out_specs=SPEC,
        compiler_params=pltpu.CompilerParams(vmem_limit_bytes=2 << 20),
        name=name,
    )(*scalars, *arrays)


def prepare(chip, core, *frames):
    spec = pl.BlockSpec(memory_space=pltpu.VMEM)
    wide = jax.ShapeDtypeStruct((3, 192, ATOMS), jnp.bfloat16)
    return pl.pallas_call(
        prepare_kernel,
        out_shape=(wide, wide, jax.ShapeDtypeStruct((8, 256), jnp.float32)),
        in_specs=[pl.BlockSpec(memory_space=pltpu.SMEM)] * 2 + [spec] * 6,
        out_specs=(spec, spec, spec),
        scratch_shapes=[pltpu.VMEM((256, 128), jnp.float32)],
        compiler_params=pltpu.CompilerParams(vmem_limit_bytes=24 << 20),
        name="prepare",
    )(chip, core, *frames)


SPEC = pl.BlockSpec(memory_space=pltpu.VMEM)
SCRATCH = [pltpu.VMEM((192, ATOMS), jnp.bfloat16), pltpu.VMEM((3, 96, 256), jnp.float32)]
TILES = jax.ShapeDtypeStruct((32, 384), jnp.float32)
MESSAGE = jax.ShapeDtypeStruct((32, 128), jnp.float32)
PACKED = jax.ShapeDtypeStruct((48, 128), jnp.float32)


def own_rows(chip, rows, high, low, norm, *more):
    return pl.pallas_call(
        own_kernel if more else early_kernel,
        out_shape=(TILES, MESSAGE) if more else TILES,
        in_specs=[pl.BlockSpec(memory_space=pltpu.SMEM)] + [SPEC] * (4 + len(more)),
        out_specs=(SPEC, SPEC) if more else SPEC,
        scratch_shapes=SCRATCH,
        compiler_params=pltpu.CompilerParams(vmem_limit_bytes=24 << 20),
        name="rows_of_own" if more else "early_rows_of_own",
    )(chip, rows, high, low, norm, *more)


def partner_rows(chip, before, *arrays):
    return pl.pallas_call(
        functools.partial(partner_kernel, before=before),
        out_shape=MESSAGE if before else PACKED,
        in_specs=[pl.BlockSpec(memory_space=pltpu.SMEM)] + [SPEC] * len(arrays),
        out_specs=SPEC,
        scratch_shapes=SCRATCH,
        compiler_params=pltpu.CompilerParams(vmem_limit_bytes=24 << 20),
        name="rows_of_partner",
    )(chip, *arrays)


def on_device(frames):
    rep = lax.axis_index("rep")
    core = rep % 2
    chip = rep // 2 * (CHIPS // 2) + lax.axis_index("blk")
    always = chip < CHIPS
    chips = range(CHIPS)
    afters = [c for c in chips if c % PLANE == 0]
    befores = [c for c in chips if c % PLANE == PLANE - 1]
    not_after = [c for c in chips if c not in afters]
    not_before = [c for c in chips if c not in befores]
    half = CHIPS // 2
    raw = frames.transpose(1, 0, 2).reshape(96, ATOMS)

    first = [(c, 1 if c % 2 else -1) for c in chips if c % PLANE]
    second = [(c, -1 if c % 2 else 1) for c in chips]
    one = stepped(raw, first)
    two = stepped(raw, second)
    far = moved(raw, half, 0, not_before)
    far_before = moved(raw, half, 0, befores)

    def swap_near(one, two, scale):
        return moved(one, 0, 1, not_before) * scale, moved(two, 0, 1) * scale

    scale = always.astype(jnp.float32)
    raw_other, then = lax.cond(
        always, lambda raw, scale: (moved(raw, 0, 1) * scale, chip), lambda raw, _: (raw, chip), raw, scale
    )
    one_other, two_other = lax.cond(then < CHIPS, swap_near, lambda one, two, _: (one, two), one, two, scale)
    place = tuple(value.reshape(1).astype(jnp.int32) for value in (chip, core))
    columns = prepare(*place, one, one_other, raw, raw_other, two, two_other)
    early = own_rows(place[0], raw, *columns)
    for_partner = partner_rows(place[0], False, far, *columns, early)
    returned = moved(for_partner, half, 0, not_before)
    own, message = own_rows(place[0], raw, *columns, early, for_partner)
    mine = moved(message, -1, 0, afters)
    other = moved(message, -1, 1, afters)
    for_partner_before = partner_rows(place[0], True, far_before, *columns, message)
    returned_before = moved(for_partner_before, half, 0, befores)
    tiles = small_call(tiles_kernel, place[:1], (own, returned), "tiles")
    tiles = small_call(next_kernel, place, (tiles, mine, other), "next_columns")
    return small_call(final_kernel, place[:1], (tiles, returned_before), "final")


def solution(mesh):
    return jax.shard_map(
        on_device,
        mesh=mesh,
        in_specs=(P(AXES, None, None),),
        out_specs=P(AXES, None),
        check_vma=False,
    )
```

```python
import functools

import jax
import jax.numpy as jnp
from jax import lax
from jax.experimental import pallas as pl
from jax.experimental.pallas import tpu as pltpu
from jax.sharding import PartitionSpec as P

ITERS = 8
ATOMS = 1024
AXES = ("blk", "rep")
CHIPS = 256
PLANE = 32


def device_of(chip, core):
    half, block = divmod(chip % CHIPS, CHIPS // 2)
    return block * 4 + half * 2 + core


def moved(value, chips, cores, senders=range(CHIPS)):
    pairs = [
        (device_of(chip, core), device_of(chip + chips, (core + cores) % 2))
        for chip in senders
        for core in range(2)
    ]
    return lax.ppermute(value, AXES, pairs)


def stepped(value, steps):
    pairs = [(device_of(chip, core), device_of(chip + step, core)) for chip, step in steps for core in range(2)]
    return lax.ppermute(value, AXES, pairs)


def centred_of(raw):
    return raw - jnp.sum(raw, axis=1, keepdims=True) * (1.0 / ATOMS)


def split(value):
    high = value.astype(jnp.bfloat16)
    low = (value - high.astype(jnp.float32)).astype(jnp.bfloat16)
    return high, low


def prepare_kernel(chip_ref, core_ref, *refs):
    frames, (high_ref, low_ref, norm_ref, column_ref) = refs[:6], refs[6:]
    core, odd = core_ref[0], chip_ref[0] % 2
    column_ref[...] = jnp.zeros_like(column_ref)
    for n, ref in enumerate(frames):
        at = core if n % 2 == 0 else 1 - core
        group = (2 * odd, 1, 2 - 2 * odd)[n // 2]
        start = pl.multiple_of(64 * group + 32 * at, 32)
        norm = jnp.zeros((32, 1), jnp.float32)
        for b in range(3):
            centred = centred_of(ref[32 * b : 32 * b + 32, :])
            norm = norm + jnp.sum(centred * centred, axis=1, keepdims=True)
            high, low = split(centred)
            high_ref[b, pl.ds(start, 32), :] = high
            low_ref[b, pl.ds(start, 32), :] = low
        column_ref[pl.ds(start, 32), :] = jnp.broadcast_to(norm, (32, 128))
    norm_ref[...] = jnp.transpose(column_ref[...])[0:8, :]


ROOT_HALF = 0.5**0.5


def polar_trace(cov, scale):
    scale = scale * ROOT_HALF
    x = [[cov[a][b] * scale for b in range(3)] for a in range(3)]
    for _ in range(ITERS):
        g = {}
        for p in range(3):
            for q in range(p, 3):
                g[p, q] = g[q, p] = x[0][p] * x[0][q] + x[1][p] * x[1][q] + x[2][p] * x[2][q]
        x = [
            [
                x[a][b] * (1.5 - g[b, b]) - (x[a][(b + 1) % 3] * g[(b + 1) % 3, b] + x[a][(b + 2) % 3] * g[(b + 2) % 3, b])
                for b in range(3)
            ]
            for a in range(3)
        ]
    return sum(x[a][b] * cov[a][b] for a in range(3) for b in range(3)) * (1.0 / ROOT_HALF)


def folded(value):
    return jnp.concatenate([value[:16], value[16:]], axis=1)


def fill_rows(rows_ref, high_ref, low_ref, norm_ref, out_ref, left_ref, cov_ref):
    norm = jnp.zeros((32, 1), jnp.float32)
    for a in range(3):
        centred = centred_of(rows_ref[32 * a : 32 * a + 32, :])
        norm = norm + jnp.sum(centred * centred, axis=1, keepdims=True)
        high, low = split(centred)
        left_ref[32 * a : 32 * a + 32, :] = high
        left_ref[96 + 32 * a : 128 + 32 * a, :] = low
    dims = (((1,), (1,)), ((), ()))
    used = 128 if out_ref.shape == (32, 128) else 192
    for b in range(3):
        one = lax.dot_general(left_ref[...], high_ref[b, :used], dims, preferred_element_type=jnp.float32)
        two = lax.dot_general(left_ref[...], low_ref[b, :used], dims, preferred_element_type=jnp.float32)
        cov_ref[b, :, :used] = one[:96] + (one[96:] + two[:96] + two[96:])

    def tile(lanes, norm, columns, shaped=lambda value: value):
        scale = (1.0 / jnp.sqrt(norm + 1e-6)) * (1.0 / jnp.sqrt(columns + 1e-6))
        cov = [[shaped(cov_ref[b, 32 * a : 32 * a + 32, lanes]) for b in range(3)] for a in range(3)]
        return (norm + columns - 2.0 * polar_trace(cov, scale)) * (1.0 / ATOMS)

    first = tile(slice(0, 128), norm, norm_ref[0:1, :128])
    if used == 128:
        out_ref[...] = first
        return
    columns = norm_ref[0:1, 128:192]
    second = tile(
        slice(128, 192),
        folded(jnp.broadcast_to(norm, (32, 64))),
        jnp.concatenate([columns, columns], axis=1),
        folded,
    )
    if out_ref.shape[1] == 128:
        out_ref[0:32, :] = first
        out_ref[32:48, :] = second
    else:
        out_ref[...] = doubled(first, jnp.concatenate([second[:, :64], second[:, 64:]], axis=0))


def doubled(first, nxt):
    prev, own = first[:, :64], first[:, 64:]
    return jnp.concatenate([prev, prev, own, own, nxt, nxt], axis=1)


def is_late(chip):
    return jnp.logical_and(chip % PLANE == 0, jnp.logical_or(chip == 0, chip // PLANE >= 3))


def early_kernel(chip_ref, rows_ref, high_ref, low_ref, norm_ref, out_ref, left_ref, cov_ref):
    late = is_late(chip_ref[0])

    @pl.when(jnp.logical_not(late))
    def _():
        fill_rows(rows_ref, high_ref, low_ref, norm_ref, out_ref, left_ref, cov_ref)

    @pl.when(late)
    def _():
        out_ref[...] = jnp.zeros_like(out_ref)


def own_kernel(chip_ref, rows_ref, high_ref, low_ref, norm_ref, early_ref, partner_ref, out_ref, message_ref, left_ref, cov_ref):
    late = is_late(chip_ref[0])

    @pl.when(late)
    def _():
        fill_rows(rows_ref, high_ref, low_ref, norm_ref, out_ref, left_ref, cov_ref)

    @pl.when(jnp.logical_not(late))
    def _():
        out_ref[...] = early_ref[...]

    message_ref[...] = jnp.concatenate([out_ref[:, :64], partner_ref[0:32, :64]], axis=1)


def partner_kernel(chip_ref, rows_ref, high_ref, low_ref, norm_ref, *refs, before):
    out_ref, left_ref, cov_ref = refs[-3:]
    here = (chip_ref[0] % PLANE == PLANE - 1) == before

    @pl.when(here)
    def _():
        fill_rows(rows_ref, high_ref, low_ref, norm_ref, out_ref, left_ref, cov_ref)

    @pl.when(jnp.logical_not(here))
    def _():
        out_ref[...] = jnp.zeros_like(out_ref)


def next_kernel(chip_ref, core_ref, own_ref, far_ref, mine_ref, other_ref, out_ref):
    chip, core = chip_ref[0], core_ref[0]
    tiles_kernel(chip_ref, own_ref, far_ref, out_ref)

    @pl.when(chip % PLANE == PLANE - 1)
    def _():
        mine, other = mine_ref[...], other_ref[...]
        zero = core == 0
        pair = jnp.concatenate([jnp.where(zero, mine, other), jnp.where(zero, other, mine)], axis=0)
        pair = jnp.concatenate([pair, pair], axis=0)
        turned = jnp.transpose(pair)[:, :64]
        same = jnp.where(zero, turned[0:32], turned[32:64])
        cross = jnp.where(zero, turned[64:96], turned[96:128])
        first = (chip + 1) % CHIPS // (CHIPS // 2) == 0
        out_ref[:, 256:384] = jnp.concatenate(
            [jnp.where(first, same, cross), jnp.where(first, cross, same)], axis=1
        )


def final_kernel(chip_ref, tiles_ref, far_ref, out_ref):
    chip = chip_ref[0]
    out_ref[...] = tiles_ref[...]

    @pl.when(chip % PLANE == PLANE - 1)
    def _():
        prev, own = far_ref[:, :64], far_ref[:, 64:]
        far = jnp.concatenate([prev, prev, own, own], axis=1)
        out_ref[:, :256] = jnp.where(is_here(chip)[:, :256], tiles_ref[:, :256], far)


def is_here(chip):
    lane = lax.broadcasted_iota(jnp.int32, (32, 384), 1)
    return (chip + (CHIPS - 1) + lane // 128) % CHIPS // (CHIPS // 2) == lane // 64 % 2


def tiles_kernel(chip_ref, own_ref, far_ref, out_ref):
    nxt = jnp.concatenate([far_ref[32:48, :64], far_ref[32:48, 64:]], axis=0)
    out_ref[...] = jnp.where(is_here(chip_ref[0]), own_ref[...], doubled(far_ref[0:32, :], nxt))


def small_call(kernel, scalars, arrays, name):
    return pl.pallas_call(
        kernel,
        out_shape=TILES,
        in_specs=[pl.BlockSpec(memory_space=pltpu.SMEM)] * len(scalars) + [SPEC] * len(arrays),
        out_specs=SPEC,
        compiler_params=pltpu.CompilerParams(vmem_limit_bytes=2 << 20),
        name=name,
    )(*scalars, *arrays)


def prepare(chip, core, *frames):
    spec = pl.BlockSpec(memory_space=pltpu.VMEM)
    wide = jax.ShapeDtypeStruct((3, 192, ATOMS), jnp.bfloat16)
    return pl.pallas_call(
        prepare_kernel,
        out_shape=(wide, wide, jax.ShapeDtypeStruct((8, 256), jnp.float32)),
        in_specs=[pl.BlockSpec(memory_space=pltpu.SMEM)] * 2 + [spec] * 6,
        out_specs=(spec, spec, spec),
        scratch_shapes=[pltpu.VMEM((256, 128), jnp.float32)],
        compiler_params=pltpu.CompilerParams(vmem_limit_bytes=24 << 20),
        name="prepare",
    )(chip, core, *frames)


SPEC = pl.BlockSpec(memory_space=pltpu.VMEM)
SCRATCH = [pltpu.VMEM((192, ATOMS), jnp.bfloat16), pltpu.VMEM((3, 96, 256), jnp.float32)]
TILES = jax.ShapeDtypeStruct((32, 384), jnp.float32)
MESSAGE = jax.ShapeDtypeStruct((32, 128), jnp.float32)
PACKED = jax.ShapeDtypeStruct((48, 128), jnp.float32)


def own_rows(chip, rows, high, low, norm, *more):
    return pl.pallas_call(
        own_kernel if more else early_kernel,
        out_shape=(TILES, MESSAGE) if more else TILES,
        in_specs=[pl.BlockSpec(memory_space=pltpu.SMEM)] + [SPEC] * (4 + len(more)),
        out_specs=(SPEC, SPEC) if more else SPEC,
        scratch_shapes=SCRATCH,
        compiler_params=pltpu.CompilerParams(vmem_limit_bytes=24 << 20),
        name="rows_of_own" if more else "early_rows_of_own",
    )(chip, rows, high, low, norm, *more)


def partner_rows(chip, before, *arrays):
    return pl.pallas_call(
        functools.partial(partner_kernel, before=before),
        out_shape=MESSAGE if before else PACKED,
        in_specs=[pl.BlockSpec(memory_space=pltpu.SMEM)] + [SPEC] * len(arrays),
        out_specs=SPEC,
        scratch_shapes=SCRATCH,
        compiler_params=pltpu.CompilerParams(vmem_limit_bytes=24 << 20),
        name="rows_of_partner",
    )(chip, *arrays)


def on_device(frames):
    rep = lax.axis_index("rep")
    core = rep % 2
    chip = rep // 2 * (CHIPS // 2) + lax.axis_index("blk")
    always = chip < CHIPS
    chips = range(CHIPS)
    afters = [c for c in chips if c % PLANE == 0]
    befores = [c for c in chips if c % PLANE == PLANE - 1]
    not_after = [c for c in chips if c not in afters]
    not_before = [c for c in chips if c not in befores]
    half = CHIPS // 2
    raw = frames.transpose(1, 0, 2).reshape(96, ATOMS)

    first = [(c, 1 if c % 2 else -1) for c in chips if c % PLANE]
    second = [(c, -1 if c % 2 else 1) for c in chips]
    one = stepped(raw, first)
    two = stepped(raw, second)
    far = moved(raw, half, 0, not_before)
    far_before = moved(raw, half, 0, befores)

    def swap_near(one, two, scale):
        return moved(one, 0, 1, not_before) * scale, moved(two, 0, 1) * scale

    scale = always.astype(jnp.float32)
    raw_other, then = lax.cond(
        always, lambda raw, scale: (moved(raw, 0, 1) * scale, chip), lambda raw, _: (raw, chip), raw, scale
    )
    one_other, two_other = lax.cond(then < CHIPS, swap_near, lambda one, two, _: (one, two), one, two, scale)
    place = tuple(value.reshape(1).astype(jnp.int32) for value in (chip, core))
    columns = prepare(*place, one, one_other, raw, raw_other, two, two_other)
    early = own_rows(place[0], raw, *columns)
    for_partner = partner_rows(place[0], False, far, *columns, early)
    returned = moved(for_partner, half, 0, not_before)
    own, message = own_rows(place[0], raw, *columns, early, for_partner)
    mine = moved(message, -1, 0, afters)
    other = moved(message, -1, 1, afters)
    for_partner_before = partner_rows(place[0], True, far_before, *columns, message)
    returned_before = moved(for_partner_before, half, 0, befores)
    tiles = small_call(next_kernel, place, (own, returned, mine, other), "next_columns")
    return small_call(final_kernel, place[:1], (tiles, returned_before), "final")


def solution(mesh):
    return jax.shard_map(
        on_device,
        mesh=mesh,
        in_specs=(P(AXES, None, None),),
        out_specs=P(AXES, None),
        check_vma=False,
    )
```

```python
import functools

import jax
import jax.numpy as jnp
from jax import lax
from jax.experimental import pallas as pl
from jax.experimental.pallas import tpu as pltpu
from jax.sharding import PartitionSpec as P

ITERS = 8
ATOMS = 1024
AXES = ("blk", "rep")
CHIPS = 256
PLANE = 32


def device_of(chip, core):
    half, block = divmod(chip % CHIPS, CHIPS // 2)
    return block * 4 + half * 2 + core


def moved(value, chips, cores, senders=range(CHIPS)):
    pairs = [
        (device_of(chip, core), device_of(chip + chips, (core + cores) % 2))
        for chip in senders
        for core in range(2)
    ]
    return lax.ppermute(value, AXES, pairs)


def stepped(value, steps):
    pairs = [(device_of(chip, core), device_of(chip + step, core)) for chip, step in steps for core in range(2)]
    return lax.ppermute(value, AXES, pairs)


def centred_of(raw):
    return raw - jnp.sum(raw, axis=1, keepdims=True) * (1.0 / ATOMS)


def split(value):
    high = value.astype(jnp.bfloat16)
    low = (value - high.astype(jnp.float32)).astype(jnp.bfloat16)
    return high, low


def prepare_kernel(chip_ref, core_ref, *refs):
    frames, (high_ref, low_ref, norm_ref, column_ref) = refs[:6], refs[6:]
    core, odd = core_ref[0], chip_ref[0] % 2
    column_ref[...] = jnp.zeros_like(column_ref)
    for n, ref in enumerate(frames):
        at = core if n % 2 == 0 else 1 - core
        group = (2 * odd, 1, 2 - 2 * odd)[n // 2]
        start = pl.multiple_of(64 * group + 32 * at, 32)
        norm = jnp.zeros((32, 1), jnp.float32)
        for b in range(3):
            centred = centred_of(ref[32 * b : 32 * b + 32, :])
            norm = norm + jnp.sum(centred * centred, axis=1, keepdims=True)
            high, low = split(centred)
            high_ref[b, pl.ds(start, 32), :] = high
            low_ref[b, pl.ds(start, 32), :] = low
        column_ref[pl.ds(start, 32), :] = jnp.broadcast_to(norm, (32, 128))
    norms = jnp.transpose(column_ref[...])[0:8, :]
    row = lax.broadcasted_iota(jnp.int32, norms.shape, 0)
    norm_ref[...] = jnp.where(row < 4, norms, 1.0 / jnp.sqrt(norms + 1e-6))


ROOT_HALF = 0.5**0.5


def polar_trace(cov, scale):
    scale = scale * ROOT_HALF
    x = [[cov[a][b] * scale for b in range(3)] for a in range(3)]
    for _ in range(ITERS):
        g = {}
        for p in range(3):
            for q in range(p, 3):
                g[p, q] = g[q, p] = x[0][p] * x[0][q] + x[1][p] * x[1][q] + x[2][p] * x[2][q]
        x = [
            [
                x[a][b] * (1.5 - g[b, b]) - (x[a][(b + 1) % 3] * g[(b + 1) % 3, b] + x[a][(b + 2) % 3] * g[(b + 2) % 3, b])
                for b in range(3)
            ]
            for a in range(3)
        ]
    return sum(x[a][b] * cov[a][b] for a in range(3) for b in range(3)) * (1.0 / ROOT_HALF)


def folded(value):
    return jnp.concatenate([value[:16], value[16:]], axis=1)


def fill_rows(rows_ref, high_ref, low_ref, norm_ref, out_ref, left_ref, cov_ref):
    norm = jnp.zeros((32, 1), jnp.float32)
    for a in range(3):
        centred = centred_of(rows_ref[32 * a : 32 * a + 32, :])
        norm = norm + jnp.sum(centred * centred, axis=1, keepdims=True)
        high, low = split(centred)
        left_ref[32 * a : 32 * a + 32, :] = high
        left_ref[96 + 32 * a : 128 + 32 * a, :] = low
    dims = (((1,), (1,)), ((), ()))
    used = 128 if out_ref.shape == (32, 128) else 192
    for b in range(3):
        one = lax.dot_general(left_ref[...], high_ref[b, :used], dims, preferred_element_type=jnp.float32)
        two = lax.dot_general(left_ref[...], low_ref[b, :used], dims, preferred_element_type=jnp.float32)
        cov_ref[b, :, :used] = one[:96] + (one[96:] + two[:96] + two[96:])

    def tile(lanes, norm, columns, roots, shaped=lambda value: value):
        scale = (1.0 / jnp.sqrt(norm + 1e-6)) * roots
        cov = [[shaped(cov_ref[b, 32 * a : 32 * a + 32, lanes]) for b in range(3)] for a in range(3)]
        return (norm + columns - 2.0 * polar_trace(cov, scale)) * (1.0 / ATOMS)

    first = tile(slice(0, 128), norm, norm_ref[0:1, :128], norm_ref[4:5, :128])
    if used == 128:
        out_ref[...] = first
        return
    columns, roots = norm_ref[0:1, 128:192], norm_ref[4:5, 128:192]
    second = tile(
        slice(128, 192),
        folded(jnp.broadcast_to(norm, (32, 64))),
        jnp.concatenate([columns, columns], axis=1),
        jnp.concatenate([roots, roots], axis=1),
        folded,
    )
    if out_ref.shape[1] == 128:
        out_ref[0:32, :] = first
        out_ref[32:48, :] = second
    else:
        out_ref[...] = doubled(first, jnp.concatenate([second[:, :64], second[:, 64:]], axis=0))


def doubled(first, nxt):
    prev, own = first[:, :64], first[:, 64:]
    return jnp.concatenate([prev, prev, own, own, nxt, nxt], axis=1)


def is_late(chip):
    return jnp.logical_and(chip % PLANE == 0, jnp.logical_or(chip == 0, chip // PLANE >= 3))


def early_kernel(chip_ref, rows_ref, high_ref, low_ref, norm_ref, out_ref, left_ref, cov_ref):
    late = is_late(chip_ref[0])

    @pl.when(jnp.logical_not(late))
    def _():
        fill_rows(rows_ref, high_ref, low_ref, norm_ref, out_ref, left_ref, cov_ref)

    @pl.when(late)
    def _():
        out_ref[...] = jnp.zeros_like(out_ref)


def own_kernel(chip_ref, rows_ref, high_ref, low_ref, norm_ref, early_ref, partner_ref, out_ref, message_ref, left_ref, cov_ref):
    late = is_late(chip_ref[0])

    @pl.when(late)
    def _():
        fill_rows(rows_ref, high_ref, low_ref, norm_ref, out_ref, left_ref, cov_ref)

    @pl.when(jnp.logical_not(late))
    def _():
        out_ref[...] = early_ref[...]

    message_ref[...] = jnp.concatenate([out_ref[:, :64], partner_ref[0:32, :64]], axis=1)


def partner_kernel(chip_ref, rows_ref, high_ref, low_ref, norm_ref, *refs, before):
    out_ref, left_ref, cov_ref = refs[-3:]
    here = (chip_ref[0] % PLANE == PLANE - 1) == before

    @pl.when(here)
    def _():
        fill_rows(rows_ref, high_ref, low_ref, norm_ref, out_ref, left_ref, cov_ref)

    @pl.when(jnp.logical_not(here))
    def _():
        out_ref[...] = jnp.zeros_like(out_ref)


def next_kernel(chip_ref, core_ref, own_ref, far_ref, mine_ref, other_ref, out_ref):
    chip, core = chip_ref[0], core_ref[0]
    tiles_kernel(chip_ref, own_ref, far_ref, out_ref)

    @pl.when(chip % PLANE == PLANE - 1)
    def _():
        mine, other = mine_ref[...], other_ref[...]
        zero = core == 0
        pair = jnp.concatenate([jnp.where(zero, mine, other), jnp.where(zero, other, mine)], axis=0)
        pair = jnp.concatenate([pair, pair], axis=0)
        turned = jnp.transpose(pair)[:, :64]
        same = jnp.where(zero, turned[0:32], turned[32:64])
        cross = jnp.where(zero, turned[64:96], turned[96:128])
        first = (chip + 1) % CHIPS // (CHIPS // 2) == 0
        out_ref[:, 256:384] = jnp.concatenate(
            [jnp.where(first, same, cross), jnp.where(first, cross, same)], axis=1
        )


def final_kernel(chip_ref, tiles_ref, far_ref, out_ref):
    chip = chip_ref[0]
    out_ref[...] = tiles_ref[...]

    @pl.when(chip % PLANE == PLANE - 1)
    def _():
        prev, own = far_ref[:, :64], far_ref[:, 64:]
        far = jnp.concatenate([prev, prev, own, own], axis=1)
        out_ref[:, :256] = jnp.where(is_here(chip)[:, :256], tiles_ref[:, :256], far)


def is_here(chip):
    lane = lax.broadcasted_iota(jnp.int32, (32, 384), 1)
    return (chip + (CHIPS - 1) + lane // 128) % CHIPS // (CHIPS // 2) == lane // 64 % 2


def tiles_kernel(chip_ref, own_ref, far_ref, out_ref):
    nxt = jnp.concatenate([far_ref[32:48, :64], far_ref[32:48, 64:]], axis=0)
    out_ref[...] = jnp.where(is_here(chip_ref[0]), own_ref[...], doubled(far_ref[0:32, :], nxt))


def small_call(kernel, scalars, arrays, name):
    return pl.pallas_call(
        kernel,
        out_shape=TILES,
        in_specs=[pl.BlockSpec(memory_space=pltpu.SMEM)] * len(scalars) + [SPEC] * len(arrays),
        out_specs=SPEC,
        compiler_params=pltpu.CompilerParams(vmem_limit_bytes=2 << 20),
        name=name,
    )(*scalars, *arrays)


def prepare(chip, core, *frames):
    spec = pl.BlockSpec(memory_space=pltpu.VMEM)
    wide = jax.ShapeDtypeStruct((3, 192, ATOMS), jnp.bfloat16)
    return pl.pallas_call(
        prepare_kernel,
        out_shape=(wide, wide, jax.ShapeDtypeStruct((8, 256), jnp.float32)),
        in_specs=[pl.BlockSpec(memory_space=pltpu.SMEM)] * 2 + [spec] * 6,
        out_specs=(spec, spec, spec),
        scratch_shapes=[pltpu.VMEM((256, 128), jnp.float32)],
        compiler_params=pltpu.CompilerParams(vmem_limit_bytes=24 << 20),
        name="prepare",
    )(chip, core, *frames)


SPEC = pl.BlockSpec(memory_space=pltpu.VMEM)
SCRATCH = [pltpu.VMEM((192, ATOMS), jnp.bfloat16), pltpu.VMEM((3, 96, 256), jnp.float32)]
TILES = jax.ShapeDtypeStruct((32, 384), jnp.float32)
MESSAGE = jax.ShapeDtypeStruct((32, 128), jnp.float32)
PACKED = jax.ShapeDtypeStruct((48, 128), jnp.float32)


def own_rows(chip, rows, high, low, norm, *more):
    return pl.pallas_call(
        own_kernel if more else early_kernel,
        out_shape=(TILES, MESSAGE) if more else TILES,
        in_specs=[pl.BlockSpec(memory_space=pltpu.SMEM)] + [SPEC] * (4 + len(more)),
        out_specs=(SPEC, SPEC) if more else SPEC,
        scratch_shapes=SCRATCH,
        compiler_params=pltpu.CompilerParams(vmem_limit_bytes=24 << 20),
        name="rows_of_own" if more else "early_rows_of_own",
    )(chip, rows, high, low, norm, *more)


def partner_rows(chip, before, *arrays):
    return pl.pallas_call(
        functools.partial(partner_kernel, before=before),
        out_shape=MESSAGE if before else PACKED,
        in_specs=[pl.BlockSpec(memory_space=pltpu.SMEM)] + [SPEC] * len(arrays),
        out_specs=SPEC,
        scratch_shapes=SCRATCH,
        compiler_params=pltpu.CompilerParams(vmem_limit_bytes=24 << 20),
        name="rows_of_partner",
    )(chip, *arrays)


def on_device(frames):
    rep = lax.axis_index("rep")
    core = rep % 2
    chip = rep // 2 * (CHIPS // 2) + lax.axis_index("blk")
    always = chip < CHIPS
    chips = range(CHIPS)
    afters = [c for c in chips if c % PLANE == 0]
    befores = [c for c in chips if c % PLANE == PLANE - 1]
    not_after = [c for c in chips if c not in afters]
    not_before = [c for c in chips if c not in befores]
    half = CHIPS // 2
    raw = frames.transpose(1, 0, 2).reshape(96, ATOMS)

    first = [(c, 1 if c % 2 else -1) for c in chips if c % PLANE]
    second = [(c, -1 if c % 2 else 1) for c in chips]
    one = stepped(raw, first)
    two = stepped(raw, second)
    far = moved(raw, half, 0, not_before)
    far_before = moved(raw, half, 0, befores)

    def swap_near(one, two, scale):
        return moved(one, 0, 1, not_before) * scale, moved(two, 0, 1) * scale

    scale = always.astype(jnp.float32)
    raw_other, then = lax.cond(
        always, lambda raw, scale: (moved(raw, 0, 1) * scale, chip), lambda raw, _: (raw, chip), raw, scale
    )
    one_other, two_other = lax.cond(then < CHIPS, swap_near, lambda one, two, _: (one, two), one, two, scale)
    place = tuple(value.reshape(1).astype(jnp.int32) for value in (chip, core))
    columns = prepare(*place, one, one_other, raw, raw_other, two, two_other)
    early = own_rows(place[0], raw, *columns)
    for_partner = partner_rows(place[0], False, far, *columns, early)
    returned = moved(for_partner, half, 0, not_before)
    own, message = own_rows(place[0], raw, *columns, early, for_partner)
    mine = moved(message, -1, 0, afters)
    other = moved(message, -1, 1, afters)
    for_partner_before = partner_rows(place[0], True, far_before, *columns, message)
    returned_before = moved(for_partner_before, half, 0, befores)
    tiles = small_call(next_kernel, place, (own, returned, mine, other), "next_columns")
    return small_call(final_kernel, place[:1], (tiles, returned_before), "final")


def solution(mesh):
    return jax.shard_map(
        on_device,
        mesh=mesh,
        in_specs=(P(AXES, None, None),),
        out_specs=P(AXES, None),
        check_vma=False,
    )
```
